32 devices in a mesh: band: 4 (over y, core), plane: 8 (over z, x).
Axes of the slice: x: 2, y: 2, z: 4, core: 2. Of those that a mesh axis runs over, the one named last changes fastest.
Arguments:
- psi: float32 [2, 4, 4096, 128], P(None, 'band', 'plane'), may hold values from -8 to 8
- potential: float32 [96, 9216], P('plane'), may hold values from 0 to 2
- stick_column: int32 [4096], P('plane'), may hold values from 0 to 9215, as said below
- stick_length: int32 [4096], P('plane'), may hold values from 0 to 49, as said below
Outputs:
- psi_new: float32 [2, 4, 4096, 128], P(None, 'band', 'plane')
- potential_new: float32 [96, 9216], P('plane')
The draws below stay inside these ranges and needn't reach their ends.
Inputs may be any that keep to these rules, and one draw needn't show every extreme that they name: `stick_column`: within each device's block of 512 slots the live sticks come first and the other slots are empty with column 0. Over all devices the live slots hold every column (mx mod 96) * 96 + (my mod 96) with mx * mx + my * my <= 576 exactly once, in an order drawn from the seed; some device's block is full and the others hold fewer. `stick_length`: A live slot's length is 2 h + 1, with h the largest whole number such that mx * mx + my * my + h * h <= 576 for its column; empty slots have length 0.
All inputs are finite; a program needn't handle non-finite values.
Results may differ from the reference program's by a relative error of at most 0.0001.
Values sent between devices are 32-bit elements; how exact they have to be, the bound alone decides.
A program may use at most 64 MiB of HBM per device.

```python
import math
import jax
import jax.numpy as jnp
import numpy as np
from jax import lax

NG = 96
RAD = 24
STICK_COEFFS = 128
BAND_DEV = 1
BAND_TOTAL = 4
SLOTS_PER_DEVICE = 512
SLOT_TOTAL = 4096
NXY = 9216


def disc_table():
    rows = np.arange(-RAD, RAD + 1)
    first, second = np.meshgrid(rows, rows, indexing='ij')
    first = first.reshape(-1)
    second = second.reshape(-1)
    room = RAD * RAD - first * first - second * second
    keep = room >= 0
    first = first[keep]
    second = second[keep]
    room = room[keep]
    height = np.array([math.isqrt(int(value)) for value in room], dtype=np.int64)
    columns = first % NG * NG + second % NG
    return (columns.astype(np.int32), (2 * height + 1).astype(np.int32))


def stick_layout(key):
    columns, lengths = disc_table()
    count = columns.shape[0]
    device_list = SLOT_TOTAL // SLOTS_PER_DEVICE
    order_key, full_key, weight_key = jax.random.split(jax.random.fold_in(key, 7), 3)
    order = jax.random.permutation(order_key, count)
    fullest = jax.random.randint(full_key, (), 0, device_list)
    device_ids = jnp.arange(device_list, dtype=jnp.int32)
    weights = jax.random.randint(weight_key, (device_list,), 2, 4)
    weights = jnp.where(device_ids == fullest, 0, weights)
    remaining = count - SLOTS_PER_DEVICE
    shares = remaining * weights // jnp.sum(weights)
    shares = jnp.minimum(shares, SLOTS_PER_DEVICE)
    shares = jnp.where(device_ids == fullest, SLOTS_PER_DEVICE, shares)
    leftover = count - jnp.sum(shares)
    spaces = SLOTS_PER_DEVICE - shares
    before = jnp.cumsum(spaces) - spaces
    shares = shares + jnp.clip(leftover - before, 0, spaces)
    starts = jnp.cumsum(shares) - shares
    slot_numbers = jnp.arange(SLOT_TOTAL, dtype=jnp.int32)
    holder = slot_numbers // SLOTS_PER_DEVICE
    within = slot_numbers % SLOTS_PER_DEVICE
    live = within < shares[holder]
    chosen = jnp.clip(starts[holder] + within, 0, count - 1)
    stick = order[chosen]
    column_ids = jnp.where(live, jnp.asarray(columns)[stick], 0).astype(jnp.int32)
    length_ids = jnp.where(live, jnp.asarray(lengths)[stick], 0).astype(jnp.int32)
    return (column_ids, length_ids)


def draw_stick_column(key, part):
    return stick_layout(key)[0]


def draw_stick_length(key, part):
    return stick_layout(key)[1]


def block_levels(own_key, dims, cuts, smallest, top_value):
    def one(position, blocks):
        draws = jax.random.uniform(jax.random.fold_in(jax.random.fold_in(own_key, 6), position), (blocks,), jnp.float32, smallest / len(cuts), top_value / len(cuts))
        return jnp.repeat(jnp.exp(draws), dims[position] // blocks).reshape((-1,) + (1,) * (len(dims) - position - 1))

    level = one(*cuts[0])
    for cut in cuts[1:]:
        level = level * one(*cut)
    return level


def gaussian(key, dims, spread, most, shards=(), kind=jnp.bfloat16):
    entries = jax.random.normal(key, dims, jnp.float32) * spread
    if len(shards) > 0:
        entries = block_levels(key, dims, shards, -0.22, 0.18) * entries
    return jnp.clip(entries, min=-most, max=most).astype(kind)


def setup_inputs(seed: int = 0) -> dict:
    seeds = jax.random.split(jax.random.key(seed), 5)
    psi = gaussian(seeds[0], (2, BAND_TOTAL, SLOT_TOTAL, STICK_COEFFS), 2.0, 8.0, ((1, 4), (2, 8)), jnp.float32)
    potential = jnp.clip(2.0 * jax.random.uniform(seeds[1], (NG, NXY), jnp.float32) ** block_levels(seeds[1], (NG, NXY), ((0, 8),), -0.2, 0.2), 0.0, 2.0)
    stick_column = draw_stick_column(jax.random.fold_in(seeds[4], 71), 0)
    stick_length = draw_stick_length(jax.random.fold_in(seeds[4], 71), 0)
    return {"psi": psi, "potential": potential, "stick_column": stick_column, "stick_length": stick_length}


TIMESTEP = 0.6
LINEAR_GAIN = 0.5
CUBIC_GAIN = 0.3


def reference(psi, potential, stick_column, stick_length):
    order = jnp.arange(STICK_COEFFS, dtype=jnp.int32)
    half = (stick_length - 1) // 2
    mask = (order[None, :] < stick_length[:, None]).astype(jnp.float32)
    first = stick_column // NG
    second = stick_column % NG
    signed_first = jnp.where(first > NG // 2, first - NG, first)
    signed_second = jnp.where(second > NG // 2, second - NG, second)
    depth = order[None, :] - half[:, None]
    kinetic = ((signed_first * signed_first + signed_second * signed_second)[:, None] + depth * depth).astype(jnp.float32) / (RAD * RAD) * mask
    wrapped = (depth % NG).astype(jnp.int32)
    leading_index = first[:, None].astype(jnp.int32)
    second_index = second[:, None].astype(jnp.int32)
    field_potential = potential.reshape(NG, NG, NG).transpose(1, 2, 0)
    norm = float(NG) ** 1.5

    def synthesis(coefficients):
        grid = jnp.zeros((NG, NG, NG), coefficients.dtype).at[leading_index, second_index, wrapped].add(coefficients)
        return jnp.fft.ifftn(grid) * norm

    def analysis(values):
        spectrum = jnp.fft.fftn(values) / norm
        return spectrum[leading_index, second_index, wrapped] * mask

    def hamiltonian(coefficients):
        return kinetic * coefficients + analysis(field_potential * synthesis(coefficients))

    def one_band(carry, pair):
        term = lax.complex(pair[0], pair[1]) * mask
        start = synthesis(term)
        total = term
        for power in range(1, 4):
            term = (-1j * (TIMESTEP / power)) * hamiltonian(term)
            total = total + term
        final = synthesis(total)
        change = jnp.real(final) ** 2 + jnp.imag(final) ** 2 - jnp.real(start) ** 2 - jnp.imag(start) ** 2
        return carry + change, jnp.stack([jnp.real(total), jnp.imag(total)])

    bands_first = jnp.moveaxis(psi, 1, 0)
    summed, coefficients = lax.scan(one_band, jnp.zeros((NG, NG, NG), jnp.float32), bands_first)
    psi_new = jnp.moveaxis(coefficients, 0, 1)
    delta = (summed / BAND_DEV).transpose(2, 0, 1).reshape(NG, NG * NG)
    potential_new = potential + LINEAR_GAIN * delta + CUBIC_GAIN * delta * delta * delta
    return psi_new, potential_new
```

```python
import math

import jax
import jax.numpy as jnp
import numpy as np
from jax import lax
from jax.experimental import pallas as pl
from jax.experimental.pallas import tpu as pltpu
from jax.sharding import PartitionSpec as P

NG = 96
RAD = 24
STICK_COEFFS = 128
BAND_DEV = 1
SIDE = 2 * RAD + 1
KY = 64
LANE = 128

HIGHEST = lax.Precision.HIGHEST
TIMESTEP = 0.6
LINEAR_GAIN = 0.5
CUBIC_GAIN = 0.3


def turning(values):
    return values.astype(jnp.float32) * (2.0 * math.pi / NG)


def signed(index):
    return jnp.where(index > NG // 2, index - NG, index)


def height_tables(lengths, planes, device_list):
    order = jnp.arange(STICK_COEFFS, dtype=jnp.int32)
    height = (
        jnp.arange(device_list, dtype=jnp.int32)[None, :] * planes
        + jnp.arange(planes, dtype=jnp.int32)[:, None]
    )
    half = (lengths - 1) // 2
    shift_angle = -turning(height.T[:, :, None] * half[None, None, :] % NG)
    shift = (jnp.cos(shift_angle), jnp.sin(shift_angle))
    mask = (order[None, :] < lengths[:, None]).astype(jnp.float32)
    return (shift, mask)


def wave_table():
    angle = 2.0 * np.pi * (np.outer(np.arange(STICK_COEFFS), np.arange(NG)) % NG) / NG
    return ((np.cos(angle) * NG**-0.5).astype(np.float32), (np.sin(angle) * NG**-0.5).astype(np.float32))


def box_tables(rows):
    freq = np.arange(SIDE) - RAD
    angle = 2.0 * np.pi * (np.outer(freq, np.arange(NG)) % NG) / NG
    cosine = np.cos(angle) * NG**-0.5
    sine = np.sin(angle) * NG**-0.5
    heights = (cosine.astype(np.float32), sine.astype(np.float32))
    out = np.zeros((2, rows, NG))
    out[0, :SIDE] = cosine
    out[1, :SIDE] = sine
    wide = np.zeros((2, KY, 2, LANE))
    wide[0, :SIDE, 0, :NG] = cosine
    wide[1, :SIDE, 0, :NG] = -sine
    wide[0, :SIDE, 1, :NG] = sine
    wide[1, :SIDE, 1, :NG] = cosine
    wide = wide.reshape(2 * KY, 2 * LANE)
    return heights, out.astype(np.float32), wide.astype(np.float32)


def thirds(values):
    first = values.astype(jnp.bfloat16)
    rest = values - first.astype(jnp.float32)
    second = rest.astype(jnp.bfloat16)
    third = (rest - second.astype(jnp.float32)).astype(jnp.bfloat16)
    return first, second, third


def place(cells_ref, count):
    slots = cells_ref.shape[-1]
    index = lax.broadcasted_iota(jnp.int32, (count, slots), 0)
    hit = index == cells_ref[0]
    return jnp.where(hit, 1.0, 0.0).astype(jnp.bfloat16)


def spread_kernel(cells_ref, values_ref, out_ref):
    hits = place(cells_ref, out_ref.shape[1])

    @pl.when(pl.program_id(0) == 0)
    def _():
        out_ref[...] = jnp.zeros_like(out_ref)

    parts = [
        lax.dot_general(part, hits, (((1,), (1,)), ((), ())), preferred_element_type=jnp.float32)
        for part in thirds(values_ref[0])
    ]
    out_ref[...] += parts[0] + parts[1] + parts[2]


def pick_kernel(cells_ref, values_ref, out_ref):
    hits = place(cells_ref, values_ref.shape[1])
    parts = [
        jnp.dot(part, hits, preferred_element_type=jnp.float32) for part in thirds(values_ref[...])
    ]
    out_ref[0] = parts[0] + parts[1] + parts[2]


def spread(cells, values, count):
    groups, rows, slots = values.shape
    return pl.pallas_call(
        spread_kernel,
        grid=(groups,),
        in_specs=[
            pl.BlockSpec((1, 1, slots), lambda i: (i, 0, 0)),
            pl.BlockSpec((1, rows, slots), lambda i: (i, 0, 0)),
        ],
        out_specs=pl.BlockSpec((rows, count), lambda i: (0, 0)),
        out_shape=jax.ShapeDtypeStruct((rows, count), jnp.float32),
        compiler_params=pltpu.CompilerParams(vmem_limit_bytes=40 << 20),
    )(cells, values)


def pick(cells, values):
    groups, _, slots = cells.shape
    rows, count = values.shape
    return pl.pallas_call(
        pick_kernel,
        grid=(groups,),
        in_specs=[
            pl.BlockSpec((1, 1, slots), lambda i: (i, 0, 0)),
            pl.BlockSpec((rows, count), lambda i: (0, 0)),
        ],
        out_specs=pl.BlockSpec((1, rows, slots), lambda i: (i, 0, 0)),
        out_shape=jax.ShapeDtypeStruct((groups, rows, slots), jnp.float32),
        compiler_params=pltpu.CompilerParams(vmem_limit_bytes=40 << 20),
    )(cells, values)


def times_i(values, half):
    return jnp.concatenate([-values[..., half:], values[..., :half]], axis=-1)


def dot(subscripts, left, right):
    return jnp.einsum(subscripts, left, right, precision=HIGHEST)


def shards(psi, potential, stick_column, stick_length):
    device_list = lax.axis_size("plane")
    planes = potential.shape[0]
    slots = stick_column.shape[0]
    rows = -(-SIDE // device_list)
    if rows > 4:
        rows = -(-rows // 8) * 8
    total_rows = rows * device_list
    count = total_rows * KY
    heights, across, wide = box_tables(total_rows)
    wave = wave_table()
    shift, mask = height_tables(stick_length, planes, device_list)

    def exchange(values):
        return lax.all_to_all(values, "plane", split_axis=0, concat_axis=0, tiled=True)

    term = psi[:, 0] * mask
    upper = [
        dot("sj,jz->zs", term[0], wave[0]) - dot("sj,jz->zs", term[1], wave[1]),
        dot("sj,jz->zs", term[0], wave[1]) + dot("sj,jz->zs", term[1], wave[0]),
    ]
    upper = [part.reshape(device_list, planes, slots) for part in upper]
    first = signed(stick_column // NG)
    second = signed(stick_column % NG)
    own_cell = jnp.where(stick_length > 0, (first + RAD) * KY + second + RAD, -1)
    packed = jnp.concatenate(
        [
            upper[0] * shift[0] - upper[1] * shift[1],
            upper[0] * shift[1] + upper[1] * shift[0],
            jnp.broadcast_to(own_cell.astype(jnp.float32), (device_list, 1, slots)),
        ],
        axis=1,
    )
    arrived = exchange(packed)
    cells = arrived[:, 2 * planes :, :].astype(jnp.int32)
    box = spread(cells, arrived[:, : 2 * planes, :], count)
    start = (
        box.reshape(2, planes, device_list, rows, KY)
        .transpose(2, 1, 3, 0, 4)
        .reshape(device_list, planes, rows, 2 * KY)
    )

    inner = np.concatenate([across[0], across[1]], axis=0)
    local = jnp.pad(potential.reshape(planes, NG, NG), ((0, 0), (0, 0), (0, LANE - NG)))
    local = jnp.concatenate([local, local], axis=2)

    def to_field(values):
        lines = values.transpose(1, 0, 2, 3).reshape(planes, total_rows, 2 * KY)
        lines = dot("pkl,lm->pkm", lines, wide)
        lines = jnp.concatenate([lines, times_i(lines, LANE)], axis=1)
        return dot("kx,pkm->pxm", inner, lines)

    def from_field(field):
        lines = jnp.concatenate([field, -times_i(field, LANE)], axis=1)
        lines = dot("xk,pxm->pkm", np.concatenate([across[0].T, across[1].T], axis=0), lines)
        lines = dot("pkm,lm->pkl", lines, wide)
        return lines.reshape(planes, device_list, rows, 2 * KY).transpose(1, 0, 2, 3)

    def modulus(field):
        return field[..., :LANE] ** 2 + field[..., LANE:] ** 2

    def up(values):
        both = jnp.concatenate([values, times_i(values, KY)], axis=0)
        return dot("kz,kxl->zxl", np.concatenate(heights, axis=0), both).reshape(
            device_list, planes, rows, 2 * KY
        )

    mx = lax.axis_index("plane") * rows + lax.broadcasted_iota(jnp.int32, (SIDE, rows, 2 * KY), 1) - RAD
    my = lax.broadcasted_iota(jnp.int32, (SIDE, rows, 2 * KY), 2) % KY - RAD
    mz = lax.broadcasted_iota(jnp.int32, (SIDE, rows, 2 * KY), 0) - RAD
    square = mx * mx + my * my + mz * mz
    inside = (square <= RAD * RAD).astype(jnp.float32)
    kinetic = square.astype(jnp.float32) / (RAD * RAD) * inside

    def down(values):
        flat = values.reshape(device_list * planes, rows, 2 * KY)
        both = jnp.concatenate([flat, -times_i(flat, KY)], axis=0)
        return dot("kz,zxl->kxl", np.concatenate(heights, axis=1), both) * inside

    def advance(applied, power):
        return -(TIMESTEP / power) * times_i(applied, KY)

    field = to_field(start)
    before = modulus(field)
    paired = jnp.concatenate([from_field(field * local), start], axis=1)
    returned = exchange(paired)
    term = down(returned[:, planes:])
    total = term
    term = advance(down(returned[:, :planes]) + kinetic * term, 1)
    total = total + term
    for power in range(2, 4):
        field = to_field(exchange(up(term)))
        returned = exchange(from_field(field * local))
        term = advance(down(returned) + kinetic * term, power)
        total = total + term
    final = exchange(up(total))
    after = modulus(to_field(final))
    flat = (
        final.reshape(device_list, planes, rows, 2, KY)
        .transpose(3, 1, 0, 2, 4)
        .reshape(2 * planes, count)
    )
    home = exchange(pick(cells, flat))
    real, imag = home[:, :planes], home[:, planes:]
    turned = [
        (real * shift[0] + imag * shift[1]).reshape(NG, slots),
        (imag * shift[0] - real * shift[1]).reshape(NG, slots),
    ]
    psi_new = jnp.stack(
        [
            (dot("zs,jz->sj", turned[0], wave[0]) + dot("zs,jz->sj", turned[1], wave[1])) * mask,
            (dot("zs,jz->sj", turned[1], wave[0]) - dot("zs,jz->sj", turned[0], wave[1])) * mask,
        ]
    )[:, None]
    change = (after - before)[..., :NG].reshape(planes, NG * NG) / BAND_DEV
    whole = lax.psum(change, "band")
    potential_new = potential + LINEAR_GAIN * whole + CUBIC_GAIN * whole * whole * whole
    return (psi_new, potential_new)


def solution(mesh):
    in_specs = (P(None, "band", "plane", None), P("plane", None), P("plane"), P("plane"))
    out_specs = (P(None, "band", "plane", None), P("plane", None))
    return jax.shard_map(shards, mesh=mesh, in_specs=in_specs, out_specs=out_specs, check_vma=False)
```

```python
import functools
import math

import jax
import jax.numpy as jnp
import numpy as np
from jax import lax
from jax.experimental import pallas as pl
from jax.experimental.pallas import tpu as pltpu
from jax.sharding import PartitionSpec as P

NG = 96
RAD = 24
STICK_COEFFS = 128
BAND_DEV = 1
SIDE = 2 * RAD + 1
KY = 64
KX = 64
KZ = 56
LANE = 128

HIGHEST = lax.Precision.HIGHEST
TIMESTEP = 0.6
LINEAR_GAIN = 0.5
CUBIC_GAIN = 0.3


def turning(values):
    return values.astype(jnp.float32) * (2.0 * math.pi / NG)


def signed(index):
    return jnp.where(index > NG // 2, index - NG, index)


def height_tables(lengths, planes, device_list):
    order = jnp.arange(STICK_COEFFS, dtype=jnp.int32)
    height = (
        jnp.arange(device_list, dtype=jnp.int32)[None, :] * planes
        + jnp.arange(planes, dtype=jnp.int32)[:, None]
    )
    half = (lengths - 1) // 2
    shift_angle = -turning(height.T[:, :, None] * half[None, None, :] % NG)
    shift = (jnp.cos(shift_angle), jnp.sin(shift_angle))
    mask = (order[None, :] < lengths[:, None]).astype(jnp.float32)
    return (shift, mask)


def wave_table():
    angle = 2.0 * np.pi * (np.outer(np.arange(STICK_COEFFS), np.arange(NG)) % NG) / NG
    return ((np.cos(angle) * NG**-0.5).astype(np.float32), (np.sin(angle) * NG**-0.5).astype(np.float32))


def row_layout(device_list):
    half = [math.isqrt(RAD * RAD - (i - RAD) ** 2) for i in range(SIDE)]
    lanes = -(-sum(2 * h + 1 for h in half) // device_list)
    lanes = -(-lanes // LANE) * LANE
    order = sorted(range(SIDE), key=lambda i: (-half[i], i))
    while True:
        used = [0] * device_list
        place = [None] * SIDE
        for i in order:
            device = min(range(device_list), key=lambda d: (used[d], d))
            place[i] = (device, used[device])
            used[device] += 2 * half[i] + 1
        if max(used) <= lanes:
            return half, place, lanes
        lanes += LANE


def height_table(planes, device_list):
    freq = np.arange(KZ) - RAD
    angle = 2.0 * np.pi * (np.outer(np.arange(NG), freq) % NG) / NG
    keep = (np.arange(KZ) < SIDE) * NG**-0.5
    cosine = np.cos(angle) * keep
    sine = np.sin(angle) * keep
    table = np.block([[cosine, -sine], [sine, cosine]]).reshape(2, device_list, planes, 2 * KZ)
    return np.ascontiguousarray(table.transpose(1, 0, 2, 3).reshape(2 * NG, 2 * KZ)).astype(np.float32)


def plane_tables():
    freq = np.arange(KX) - RAD
    angle = 2.0 * np.pi * (np.outer(freq, np.arange(NG)) % NG) / NG
    keep = (np.arange(KX) < SIDE)[:, None] * NG**-0.5
    cosine = np.cos(angle) * keep
    sine = np.sin(angle) * keep
    inner = np.concatenate([cosine, sine], axis=0).T
    outer = np.concatenate([cosine, sine], axis=1)
    lines = np.zeros((LANE, 2, LANE))
    lines[:KY, 0, :NG] = cosine
    lines[:KY, 1, :NG] = sine
    back = np.zeros((2, LANE, 2, LANE))
    back[0, :NG, 0, :KY] = cosine.T
    back[1, :NG, 0, :KY] = sine.T
    back[0, :NG, 1, :KY] = -sine.T
    back[1, :NG, 1, :KY] = cosine.T
    return (
        np.ascontiguousarray(inner).astype(np.float32),
        outer.astype(np.float32),
        lines.reshape(LANE, 2 * LANE).astype(np.float32),
        back.reshape(2 * LANE, 2 * LANE).astype(np.float32),
    )


def thirds(values):
    first = values.astype(jnp.bfloat16).astype(jnp.float32)
    rest = values - first
    second = rest.astype(jnp.bfloat16).astype(jnp.float32)
    return jnp.concatenate([first, second, rest - second], axis=0).astype(jnp.bfloat16)


def add_thirds(parts):
    rows = parts.shape[0] // 3
    return parts[:rows] + parts[rows : 2 * rows] + parts[2 * rows :]


def spread_kernel(cells_ref, values_ref, out_ref):
    groups, rows, lanes = out_ref.shape
    slots = cells_ref.shape[1]
    index = lax.broadcasted_iota(jnp.int32, (slots, groups * lanes), 1)
    hits = jnp.where(index == cells_ref[0], 1.0, 0.0).astype(jnp.bfloat16)

    @pl.when(pl.program_id(0) == 0)
    def _():
        out_ref[...] = jnp.zeros_like(out_ref)

    parts = jnp.dot(thirds(values_ref[0]), hits, preferred_element_type=jnp.float32)
    whole = add_thirds(parts)
    for group in range(groups):
        out_ref[group] += whole[:rows, group * lanes : (group + 1) * lanes]


def pick_kernel(cells_ref, values_ref, out_ref):
    slots = cells_ref.shape[2]
    index = lax.broadcasted_iota(jnp.int32, (values_ref.shape[1], slots), 0)
    hits = jnp.where(index == cells_ref[0], 1.0, 0.0).astype(jnp.bfloat16)
    parts = jnp.dot(thirds(values_ref[...]), hits, preferred_element_type=jnp.float32)
    out_ref[0] = add_thirds(parts)[: out_ref.shape[1]]


def spread(cells, values, groups, lanes):
    sources, rows, slots = values.shape
    padded = -(-rows // 8) * 8
    values = jnp.pad(values, ((0, 0), (0, padded - rows), (0, 0)))
    return pl.pallas_call(
        spread_kernel,
        grid=(sources,),
        in_specs=[
            pl.BlockSpec((1, slots, 1), lambda i: (i, 0, 0)),
            pl.BlockSpec((1, padded, slots), lambda i: (i, 0, 0)),
        ],
        out_specs=pl.BlockSpec((groups, rows, lanes), lambda i: (0, 0, 0)),
        out_shape=jax.ShapeDtypeStruct((groups, rows, lanes), jnp.float32),
        compiler_params=pltpu.CompilerParams(vmem_limit_bytes=40 << 20),
    )(cells[:, :, None], values)


def pick(cells, values):
    sources, slots = cells.shape
    rows, count = values.shape
    padded = -(-rows // 8) * 8
    values = jnp.pad(values, ((0, padded - rows), (0, 0)))
    return pl.pallas_call(
        pick_kernel,
        grid=(sources,),
        in_specs=[
            pl.BlockSpec((1, 1, slots), lambda i: (i, 0, 0)),
            pl.BlockSpec((padded, count), lambda i: (0, 0)),
        ],
        out_specs=pl.BlockSpec((1, rows, slots), lambda i: (i, 0, 0)),
        out_shape=jax.ShapeDtypeStruct((sources, rows, slots), jnp.float32),
        compiler_params=pltpu.CompilerParams(vmem_limit_bytes=40 << 20),
    )(cells[:, None, :], values)


def product(left, right):
    return jnp.dot(left, right, precision=HIGHEST, preferred_element_type=jnp.float32)


def plane_kernel(layout, pitch, with_modulus, with_back, *refs):
    half, place, _ = layout
    arrived_ref, local_ref, inner_ref, outer_ref, lines_ref, back_ref = refs[:6]
    refs = refs[6:]
    if with_back:
        out_ref, refs = refs[0], refs[1:]
    if with_modulus:
        modulus_ref, refs = refs[0], refs[1:]
    box, cosine_part, sine_part = refs
    planes = local_ref.shape[0]
    rows = 2 * planes
    box[...] = jnp.zeros_like(box)
    for i in range(SIDE):
        device, lane = place[i]
        width = 2 * half[i] + 1
        box[i * pitch : i * pitch + rows, RAD - half[i] : RAD + half[i] + 1] = arrived_ref[
            device, :, lane : lane + width
        ]
    turned = product(box[...], lines_ref[...])
    cosine_part[...] = turned[:, :LANE]
    sine_part[...] = turned[:, LANE:]
    for p in range(planes):
        real = pl.ds(p, KX, stride=pitch)
        imag = pl.ds(planes + p, KX, stride=pitch)
        line_real = cosine_part[real, :] - sine_part[imag, :]
        line_imag = sine_part[real, :] + cosine_part[imag, :]
        lines = jnp.concatenate(
            [
                jnp.concatenate([line_real, line_imag], axis=1),
                jnp.concatenate([-line_imag, line_real], axis=1),
            ],
            axis=0,
        )
        field = product(inner_ref[...], lines)
        field_real, field_imag = field[:, :LANE], field[:, LANE:]
        if with_modulus:
            modulus_ref[p] = field_real * field_real + field_imag * field_imag
        if with_back:
            field_real = field_real * local_ref[p]
            field_imag = field_imag * local_ref[p]
            both = jnp.concatenate(
                [
                    jnp.concatenate([field_real, field_imag], axis=1),
                    jnp.concatenate([field_imag, -field_real], axis=1),
                ],
                axis=0,
            )
            result = product(product(outer_ref[...], both), back_ref[...])
            cosine_part[real, :] = result[:, :LANE]
            cosine_part[imag, :] = result[:, LANE:]
    if with_back:
        out_ref[...] = jnp.zeros_like(out_ref)
        for i in range(SIDE):
            device, lane = place[i]
            width = 2 * half[i] + 1
            out_ref[device, :, lane : lane + width] = cosine_part[
                i * pitch : i * pitch + rows, RAD - half[i] : RAD + half[i] + 1
            ]


def plane_step(layout, arrived, local, tables, with_modulus, with_back):
    planes = local.shape[0]
    pitch = -(-2 * planes // 8) * 8
    shapes = []
    if with_back:
        shapes.append(jax.ShapeDtypeStruct(arrived.shape, jnp.float32))
    if with_modulus:
        shapes.append(jax.ShapeDtypeStruct(local.shape, jnp.float32))
    kernel = functools.partial(plane_kernel, layout, pitch, with_modulus, with_back)
    whole = pl.BlockSpec(memory_space=pltpu.VMEM)
    return pl.pallas_call(
        kernel,
        in_specs=[whole] * 6,
        out_specs=[whole] * len(shapes),
        out_shape=shapes,
        scratch_shapes=[pltpu.VMEM((KX * pitch, LANE), jnp.float32)] * 3,
        compiler_params=pltpu.CompilerParams(vmem_limit_bytes=40 << 20),
    )(arrived, local, *tables)


def height_kernel(factor, last, returned_ref, term_ref, total_ref, kinetic_ref, inside_ref, table_ref, turned_ref, *refs):
    table = table_ref[...]
    applied = product(turned_ref[...], returned_ref[...]) * inside_ref[...]
    applied = applied + kinetic_ref[...] * term_ref[...]
    term = factor * jnp.concatenate([applied[KZ:], -applied[:KZ]], axis=0)
    total = total_ref[...] + term
    refs[0][...] = product(table, total if last else term)
    if not last:
        refs[1][...] = term
        refs[2][...] = total


def height_step(factor, last, returned, term, total, kinetic, inside, table):
    lanes = term.shape[1]
    shapes = [jax.ShapeDtypeStruct((table.shape[0], lanes), jnp.float32)]
    if not last:
        shapes += [jax.ShapeDtypeStruct(term.shape, jnp.float32)] * 2
    whole = pl.BlockSpec(memory_space=pltpu.VMEM)
    return pl.pallas_call(
        functools.partial(height_kernel, factor, last),
        in_specs=[whole] * 7,
        out_specs=[whole] * len(shapes),
        out_shape=shapes,
        compiler_params=pltpu.CompilerParams(vmem_limit_bytes=40 << 20),
    )(returned, term, total, kinetic, inside, table, np.ascontiguousarray(table.T))


def dot(subscripts, left, right):
    return jnp.einsum(subscripts, left, right, precision=HIGHEST)


def shards(psi, potential, stick_column, stick_length):
    device_list = lax.axis_size("plane")
    planes = potential.shape[0]
    slots = stick_column.shape[0]
    layout = row_layout(device_list)
    half, place, lanes = layout
    wave = wave_table()
    shift, mask = height_tables(stick_length, planes, device_list)

    def exchange(values):
        return lax.all_to_all(values, "plane", split_axis=0, concat_axis=0, tiled=True)

    term = psi[:, 0] * mask
    upper = [
        dot("sj,jz->zs", term[0], wave[0]) - dot("sj,jz->zs", term[1], wave[1]),
        dot("sj,jz->zs", term[0], wave[1]) + dot("sj,jz->zs", term[1], wave[0]),
    ]
    upper = [part.reshape(device_list, planes, slots) for part in upper]
    first = signed(stick_column // NG)
    second = signed(stick_column % NG)
    base = np.array([place[i][0] * lanes + place[i][1] + half[i] for i in range(SIDE)], np.int32)
    chosen = first[None, :] + RAD == jnp.arange(SIDE, dtype=jnp.int32)[:, None]
    own_cell = jnp.sum(jnp.where(chosen, base[:, None], 0), axis=0) + second
    own_cell = jnp.where(stick_length > 0, own_cell, -1)
    packed = jnp.concatenate(
        [
            upper[0] * shift[0] - upper[1] * shift[1],
            upper[0] * shift[1] + upper[1] * shift[0],
            jnp.broadcast_to(own_cell.astype(jnp.float32), (device_list, 1, slots)),
        ],
        axis=1,
    )
    arrived = exchange(packed)
    cells = arrived[:, 2 * planes, :].astype(jnp.int32)
    start = spread(cells, arrived[:, : 2 * planes, :], device_list, lanes)

    local = jnp.pad(potential.reshape(planes, NG, NG), ((0, 0), (0, 0), (0, LANE - NG)))
    tables = plane_tables()
    table = height_table(planes, device_list)
    planar = np.full((device_list, lanes), 4 * RAD * RAD, np.int32)
    for i in range(SIDE):
        device, lane = place[i]
        spot = np.arange(-half[i], half[i] + 1)
        planar[device, lane : lane + 2 * half[i] + 1] = (i - RAD) ** 2 + spot * spot
    planar = lax.dynamic_slice_in_dim(jnp.asarray(planar), lax.axis_index("plane"), 1, 0)
    depth = np.concatenate([np.arange(KZ) - RAD] * 2).astype(np.int32)[:, None]
    square = planar + depth * depth
    inside = (square <= RAD * RAD).astype(jnp.float32)
    kinetic = square.astype(jnp.float32) / (RAD * RAD) * inside

    spectrum, before = plane_step(layout, start, local, tables, True, True)
    returned = exchange(jnp.concatenate([spectrum, start], axis=1))
    shape = (2 * NG, lanes)
    term = dot("zk,zl->kl", table, returned[:, 2 * planes :].reshape(shape)) * inside
    total = term
    returned = returned[:, : 2 * planes]
    for power in range(1, 4):
        if power > 1:
            (spectrum,) = plane_step(layout, exchange(upper.reshape(start.shape)), local, tables, False, True)
            returned = exchange(spectrum)
        made = height_step(
            TIMESTEP / power, power == 3, returned.reshape(shape), term, total, kinetic, inside, table
        )
        if power < 3:
            upper, term, total = made
        else:
            upper = made[0]
    final = exchange(upper.reshape(start.shape))
    (after,) = plane_step(layout, final, local, tables, True, False)
    flat = final.transpose(1, 0, 2).reshape(2 * planes, device_list * lanes)
    home = exchange(pick(cells, flat))
    real, imag = home[:, :planes], home[:, planes:]
    turned = [
        (real * shift[0] + imag * shift[1]).reshape(NG, slots),
        (imag * shift[0] - real * shift[1]).reshape(NG, slots),
    ]
    psi_new = jnp.stack(
        [
            (dot("zs,jz->sj", turned[0], wave[0]) + dot("zs,jz->sj", turned[1], wave[1])) * mask,
            (dot("zs,jz->sj", turned[1], wave[0]) - dot("zs,jz->sj", turned[0], wave[1])) * mask,
        ]
    )[:, None]
    change = (after - before)[..., :NG].reshape(planes, NG * NG) / BAND_DEV
    whole = lax.psum(change, "band")
    potential_new = potential + LINEAR_GAIN * whole + CUBIC_GAIN * whole * whole * whole
    return (psi_new, potential_new)


def solution(mesh):
    in_specs = (P(None, "band", "plane", None), P("plane", None), P("plane"), P("plane"))
    out_specs = (P(None, "band", "plane", None), P("plane", None))
    return jax.shard_map(shards, mesh=mesh, in_specs=in_specs, out_specs=out_specs, check_vma=False)
```

```python
import functools
import math

import jax
import jax.numpy as jnp
import numpy as np
from jax import lax
from jax.experimental import pallas as pl
from jax.experimental.pallas import tpu as pltpu
from jax.sharding import PartitionSpec as P

NG = 96
RAD = 24
STICK_COEFFS = 128
BAND_DEV = 1
SIDE = 2 * RAD + 1
KY = 64
KX = 64
KZ = 56
LANE = 128

HIGHEST = lax.Precision.HIGHEST
TIMESTEP = 0.6
LINEAR_GAIN = 0.5
CUBIC_GAIN = 0.3


def turning(values):
    return values.astype(jnp.float32) * (2.0 * math.pi / NG)


def signed(index):
    return jnp.where(index > NG // 2, index - NG, index)


def height_tables(lengths, planes, device_list):
    order = jnp.arange(STICK_COEFFS, dtype=jnp.int32)
    height = (
        jnp.arange(device_list, dtype=jnp.int32)[None, :] * planes
        + jnp.arange(planes, dtype=jnp.int32)[:, None]
    )
    half = (lengths - 1) // 2
    shift_angle = -turning(height.T[:, :, None] * half[None, None, :] % NG)
    shift = (jnp.cos(shift_angle), jnp.sin(shift_angle))
    mask = (order[None, :] < lengths[:, None]).astype(jnp.float32)
    return (shift, mask)


def wave_table():
    angle = 2.0 * np.pi * (np.outer(np.arange(STICK_COEFFS), np.arange(NG)) % NG) / NG
    return ((np.cos(angle) * NG**-0.5).astype(np.float32), (np.sin(angle) * NG**-0.5).astype(np.float32))


def row_layout(device_list):
    half = [math.isqrt(RAD * RAD - (i - RAD) ** 2) for i in range(SIDE)]
    lanes = -(-sum(2 * h + 1 for h in half) // device_list)
    lanes = -(-lanes // LANE) * LANE
    order = sorted(range(SIDE), key=lambda i: (-half[i], i))
    while True:
        used = [0] * device_list
        place = [None] * SIDE
        for i in order:
            device = min(range(device_list), key=lambda d: (used[d], d))
            place[i] = (device, used[device])
            used[device] += 2 * half[i] + 1
        if max(used) <= lanes:
            return half, place, lanes
        lanes += LANE


def height_table(planes, device_list):
    freq = np.arange(KZ) - RAD
    angle = 2.0 * np.pi * (np.outer(np.arange(NG), freq) % NG) / NG
    keep = (np.arange(KZ) < SIDE) * NG**-0.5
    cosine = np.cos(angle) * keep
    sine = np.sin(angle) * keep
    table = np.block([[cosine, -sine], [sine, cosine]]).reshape(2, device_list, planes, 2 * KZ)
    return np.ascontiguousarray(table.transpose(1, 0, 2, 3).reshape(2 * NG, 2 * KZ)).astype(np.float32)


def plane_tables():
    freq = np.arange(KX) - RAD
    angle = 2.0 * np.pi * (np.outer(freq, np.arange(NG)) % NG) / NG
    keep = (np.arange(KX) < SIDE)[:, None] * NG**-0.5
    cosine = np.cos(angle) * keep
    sine = np.sin(angle) * keep
    inner = np.concatenate([cosine, sine], axis=0).T
    outer = np.concatenate([cosine, sine], axis=1)
    lines = np.zeros((LANE, 2, LANE))
    lines[:KY, 0, :NG] = cosine
    lines[:KY, 1, :NG] = sine
    back = np.zeros((2, LANE, 2, LANE))
    back[0, :NG, 0, :KY] = cosine.T
    back[1, :NG, 0, :KY] = sine.T
    back[0, :NG, 1, :KY] = -sine.T
    back[1, :NG, 1, :KY] = cosine.T
    return (
        np.ascontiguousarray(inner).astype(np.float32),
        outer.astype(np.float32),
        lines.reshape(LANE, 2 * LANE).astype(np.float32),
        back.reshape(2 * LANE, 2 * LANE).astype(np.float32),
    )


def thirds(values):
    first = values.astype(jnp.bfloat16).astype(jnp.float32)
    rest = values - first
    second = rest.astype(jnp.bfloat16).astype(jnp.float32)
    return jnp.concatenate([first, second, rest - second], axis=0).astype(jnp.bfloat16)


def add_thirds(parts):
    rows = parts.shape[0] // 3
    return parts[:rows] + parts[rows : 2 * rows] + parts[2 * rows :]


def spread_kernel(cells_ref, values_ref, out_ref):
    groups, rows, lanes = out_ref.shape
    slots = cells_ref.shape[1]
    index = lax.broadcasted_iota(jnp.int32, (slots, groups * lanes), 1)
    hits = jnp.where(index == cells_ref[0], 1.0, 0.0).astype(jnp.bfloat16)

    @pl.when(pl.program_id(0) == 0)
    def _():
        out_ref[...] = jnp.zeros_like(out_ref)

    parts = jnp.dot(thirds(values_ref[0]), hits, preferred_element_type=jnp.float32)
    whole = add_thirds(parts)
    for group in range(groups):
        out_ref[group] += whole[:rows, group * lanes : (group + 1) * lanes]


def pick_kernel(cells_ref, values_ref, out_ref):
    slots = cells_ref.shape[2]
    index = lax.broadcasted_iota(jnp.int32, (values_ref.shape[1], slots), 0)
    hits = jnp.where(index == cells_ref[0], 1.0, 0.0).astype(jnp.bfloat16)
    parts = jnp.dot(thirds(values_ref[...]), hits, preferred_element_type=jnp.float32)
    out_ref[0] = add_thirds(parts)[: out_ref.shape[1]]


def spread(cells, values, groups, lanes):
    sources, rows, slots = values.shape
    padded = -(-rows // 8) * 8
    values = jnp.pad(values, ((0, 0), (0, padded - rows), (0, 0)))
    return pl.pallas_call(
        spread_kernel,
        grid=(sources,),
        in_specs=[
            pl.BlockSpec((1, slots, 1), lambda i: (i, 0, 0)),
            pl.BlockSpec((1, padded, slots), lambda i: (i, 0, 0)),
        ],
        out_specs=pl.BlockSpec((groups, rows, lanes), lambda i: (0, 0, 0)),
        out_shape=jax.ShapeDtypeStruct((groups, rows, lanes), jnp.float32),
        compiler_params=pltpu.CompilerParams(vmem_limit_bytes=40 << 20),
    )(cells[:, :, None], values)


def pick(cells, values):
    sources, slots = cells.shape
    rows, count = values.shape
    padded = -(-rows // 8) * 8
    values = jnp.pad(values, ((0, padded - rows), (0, 0)))
    return pl.pallas_call(
        pick_kernel,
        grid=(sources,),
        in_specs=[
            pl.BlockSpec((1, 1, slots), lambda i: (i, 0, 0)),
            pl.BlockSpec((padded, count), lambda i: (0, 0)),
        ],
        out_specs=pl.BlockSpec((1, rows, slots), lambda i: (i, 0, 0)),
        out_shape=jax.ShapeDtypeStruct((sources, rows, slots), jnp.float32),
        compiler_params=pltpu.CompilerParams(vmem_limit_bytes=40 << 20),
    )(cells[:, None, :], values)


def product(left, right):
    return jnp.dot(left, right, precision=HIGHEST, preferred_element_type=jnp.float32)


def halves(values):
    first = values.astype(jnp.bfloat16)
    return first, (values - first.astype(jnp.float32)).astype(jnp.bfloat16)


def product_halves(left, right):
    def one(a, b):
        return jnp.dot(a, b, preferred_element_type=jnp.float32)

    return one(left[0], right[0]) + (one(left[0], right[1]) + one(left[1], right[0]))


def plane_kernel(layout, pitch, with_modulus, with_back, *refs):
    half, place, _ = layout
    arrived_ref, local_ref, inner_ref, outer_ref, lines_ref, back_ref = refs[:6]
    refs = refs[6:]
    if with_back:
        out_ref, refs = refs[0], refs[1:]
    if with_modulus:
        modulus_ref, refs = refs[0], refs[1:]
    box, cosine_part, sine_part = refs
    planes = local_ref.shape[0]
    rows = 2 * planes
    box[...] = jnp.zeros_like(box)
    for i in range(SIDE):
        device, lane = place[i]
        width = 2 * half[i] + 1
        box[i * pitch : i * pitch + rows, RAD - half[i] : RAD + half[i] + 1] = arrived_ref[
            device, :, lane : lane + width
        ]
    inner, outer = halves(inner_ref[...]), halves(outer_ref[...])
    turned = product_halves(halves(box[...]), halves(lines_ref[...]))
    cosine_part[...] = turned[:, :LANE]
    sine_part[...] = turned[:, LANE:]
    group = max(size for size in range(1, 5) if planes % size == 0)
    for begin in range(0, planes, group):
        top, bottom = [], []
        for p in range(begin, begin + group):
            real = pl.ds(p, KX, stride=pitch)
            imag = pl.ds(planes + p, KX, stride=pitch)
            line_real = cosine_part[real, :] - sine_part[imag, :]
            line_imag = sine_part[real, :] + cosine_part[imag, :]
            top += [line_real, line_imag]
            bottom += [-line_imag, line_real]
        lines = jnp.concatenate(
            [jnp.concatenate(top, axis=1), jnp.concatenate(bottom, axis=1)], axis=0
        )
        field = product_halves(inner, halves(lines))
        top, bottom = [], []
        for q in range(group):
            p = begin + q
            field_real = field[:, 2 * q * LANE : (2 * q + 1) * LANE]
            field_imag = field[:, (2 * q + 1) * LANE : (2 * q + 2) * LANE]
            if with_modulus:
                modulus_ref[p] = field_real * field_real + field_imag * field_imag
            if with_back:
                field_real = field_real * local_ref[p]
                field_imag = field_imag * local_ref[p]
                top += [field_real, field_imag]
                bottom += [field_imag, -field_real]
        if with_back:
            both = jnp.concatenate(
                [jnp.concatenate(top, axis=1), jnp.concatenate(bottom, axis=1)], axis=0
            )
            result = product_halves(outer, halves(both))
            result = jnp.concatenate(
                [result[:, 2 * q * LANE : (2 * q + 2) * LANE] for q in range(group)], axis=0
            )
            result = product_halves(halves(result), halves(back_ref[...]))
            for q in range(group):
                p = begin + q
                part = result[q * KX : (q + 1) * KX]
                box[pl.ds(p, KX, stride=pitch), :] = part[:, :LANE]
                box[pl.ds(planes + p, KX, stride=pitch), :] = part[:, LANE:]
    if with_back:
        out_ref[...] = jnp.zeros_like(out_ref)
        for i in range(SIDE):
            device, lane = place[i]
            width = 2 * half[i] + 1
            out_ref[device, :, lane : lane + width] = box[
                i * pitch : i * pitch + rows, RAD - half[i] : RAD + half[i] + 1
            ]


def plane_step(layout, arrived, local, tables, with_modulus, with_back):
    planes = local.shape[0]
    pitch = -(-2 * planes // 8) * 8
    shapes = []
    if with_back:
        shapes.append(jax.ShapeDtypeStruct(arrived.shape, jnp.float32))
    if with_modulus:
        shapes.append(jax.ShapeDtypeStruct(local.shape, jnp.float32))
    kernel = functools.partial(plane_kernel, layout, pitch, with_modulus, with_back)
    whole = pl.BlockSpec(memory_space=pltpu.VMEM)
    return pl.pallas_call(
        kernel,
        in_specs=[whole] * 6,
        out_specs=[whole] * len(shapes),
        out_shape=shapes,
        scratch_shapes=[pltpu.VMEM((KX * pitch, LANE), jnp.float32)] * 3,
        compiler_params=pltpu.CompilerParams(vmem_limit_bytes=40 << 20),
    )(arrived, local, *tables)


def height_kernel(factor, last, returned_ref, term_ref, total_ref, kinetic_ref, inside_ref, table_ref, turned_ref, *refs):
    table = table_ref[...]
    applied = product(turned_ref[...], returned_ref[...]) * inside_ref[...]
    applied = applied + kinetic_ref[...] * term_ref[...]
    term = factor * jnp.concatenate([applied[KZ:], -applied[:KZ]], axis=0)
    total = total_ref[...] + term
    refs[0][...] = product(table, total if last else term)
    if not last:
        refs[1][...] = term
        refs[2][...] = total


def height_step(factor, last, returned, term, total, kinetic, inside, table):
    lanes = term.shape[1]
    shapes = [jax.ShapeDtypeStruct((table.shape[0], lanes), jnp.float32)]
    if not last:
        shapes += [jax.ShapeDtypeStruct(term.shape, jnp.float32)] * 2
    whole = pl.BlockSpec(memory_space=pltpu.VMEM)
    return pl.pallas_call(
        functools.partial(height_kernel, factor, last),
        in_specs=[whole] * 7,
        out_specs=[whole] * len(shapes),
        out_shape=shapes,
        compiler_params=pltpu.CompilerParams(vmem_limit_bytes=40 << 20),
    )(returned, term, total, kinetic, inside, table, np.ascontiguousarray(table.T))


def dot(subscripts, left, right):
    return jnp.einsum(subscripts, left, right, precision=HIGHEST)


def sum_bands(values):
    bands = lax.axis_size("band")
    if bands & (bands - 1):
        return lax.psum(values, "band")
    step = 1
    while step < bands:
        pairs = [(i, i ^ step) for i in range(bands)]
        values = values + lax.ppermute(values, "band", pairs)
        step *= 2
    return values


def shards(psi, potential, stick_column, stick_length):
    device_list = lax.axis_size("plane")
    planes = potential.shape[0]
    slots = stick_column.shape[0]
    layout = row_layout(device_list)
    half, place, lanes = layout
    wave = wave_table()
    shift, mask = height_tables(stick_length, planes, device_list)

    def exchange(values):
        return lax.all_to_all(values, "plane", split_axis=0, concat_axis=0, tiled=True)

    term = psi[:, 0] * mask
    upper = [
        dot("sj,jz->zs", term[0], wave[0]) - dot("sj,jz->zs", term[1], wave[1]),
        dot("sj,jz->zs", term[0], wave[1]) + dot("sj,jz->zs", term[1], wave[0]),
    ]
    upper = [part.reshape(device_list, planes, slots) for part in upper]
    first = signed(stick_column // NG)
    second = signed(stick_column % NG)
    base = np.array([place[i][0] * lanes + place[i][1] + half[i] for i in range(SIDE)], np.int32)
    chosen = first[None, :] + RAD == jnp.arange(SIDE, dtype=jnp.int32)[:, None]
    own_cell = jnp.sum(jnp.where(chosen, base[:, None], 0), axis=0) + second
    own_cell = jnp.where(stick_length > 0, own_cell, -1)
    packed = jnp.concatenate(
        [
            upper[0] * shift[0] - upper[1] * shift[1],
            upper[0] * shift[1] + upper[1] * shift[0],
            jnp.broadcast_to(own_cell.astype(jnp.float32), (device_list, 1, slots)),
        ],
        axis=1,
    )
    arrived = exchange(packed)
    cells = arrived[:, 2 * planes, :].astype(jnp.int32)
    start = spread(cells, arrived[:, : 2 * planes, :], device_list, lanes)

    local = jnp.pad(potential.reshape(planes, NG, NG), ((0, 0), (0, 0), (0, LANE - NG)))
    tables = plane_tables()
    table = height_table(planes, device_list)
    planar = np.full((device_list, lanes), 4 * RAD * RAD, np.int32)
    for i in range(SIDE):
        device, lane = place[i]
        spot = np.arange(-half[i], half[i] + 1)
        planar[device, lane : lane + 2 * half[i] + 1] = (i - RAD) ** 2 + spot * spot
    planar = lax.dynamic_slice_in_dim(jnp.asarray(planar), lax.axis_index("plane"), 1, 0)
    depth = np.concatenate([np.arange(KZ) - RAD] * 2).astype(np.int32)[:, None]
    square = planar + depth * depth
    inside = (square <= RAD * RAD).astype(jnp.float32)
    kinetic = square.astype(jnp.float32) / (RAD * RAD) * inside

    spectrum, before = plane_step(layout, start, local, tables, True, True)
    returned = exchange(jnp.concatenate([spectrum, start], axis=1))
    shape = (2 * NG, lanes)
    term = dot("zk,zl->kl", table, returned[:, 2 * planes :].reshape(shape)) * inside
    total = term
    returned = returned[:, : 2 * planes]
    for power in range(1, 4):
        if power > 1:
            (spectrum,) = plane_step(layout, exchange(upper.reshape(start.shape)), local, tables, False, True)
            returned = exchange(spectrum)
        made = height_step(
            TIMESTEP / power, power == 3, returned.reshape(shape), term, total, kinetic, inside, table
        )
        if power < 3:
            upper, term, total = made
        else:
            upper = made[0]
    final = exchange(upper.reshape(start.shape))
    (after,) = plane_step(layout, final, local, tables, True, False)
    flat = final.transpose(1, 0, 2).reshape(2 * planes, device_list * lanes)
    home = exchange(pick(cells, flat))
    real, imag = home[:, :planes], home[:, planes:]
    turned = [
        (real * shift[0] + imag * shift[1]).reshape(NG, slots),
        (imag * shift[0] - real * shift[1]).reshape(NG, slots),
    ]
    psi_new = jnp.stack(
        [
            (dot("zs,jz->sj", turned[0], wave[0]) + dot("zs,jz->sj", turned[1], wave[1])) * mask,
            (dot("zs,jz->sj", turned[1], wave[0]) - dot("zs,jz->sj", turned[0], wave[1])) * mask,
        ]
    )[:, None]
    change = (after - before)[..., :NG].reshape(planes, NG * NG) / BAND_DEV
    whole = sum_bands(change)
    potential_new = potential + LINEAR_GAIN * whole + CUBIC_GAIN * whole * whole * whole
    return (psi_new, potential_new)


def solution(mesh):
    in_specs = (P(None, "band", "plane", None), P("plane", None), P("plane"), P("plane"))
    out_specs = (P(None, "band", "plane", None), P("plane", None))
    return jax.shard_map(shards, mesh=mesh, in_specs=in_specs, out_specs=out_specs, check_vma=False)
```

```python
import functools
import math

import jax
import jax.numpy as jnp
import numpy as np
from jax import lax
from jax.experimental import pallas as pl
from jax.experimental.pallas import tpu as pltpu
from jax.sharding import PartitionSpec as P

NG = 96
RAD = 24
STICK_COEFFS = 128
BAND_DEV = 1
SIDE = 2 * RAD + 1
KY = 64
KX = 64
KZ = 56
LANE = 128

HIGHEST = lax.Precision.HIGHEST
TIMESTEP = 0.6
LINEAR_GAIN = 0.5
CUBIC_GAIN = 0.3


def turning(values):
    return values.astype(jnp.float32) * (2.0 * math.pi / NG)


def signed(index):
    return jnp.where(index > NG // 2, index - NG, index)


def height_tables(lengths, planes, device_list):
    order = jnp.arange(STICK_COEFFS, dtype=jnp.int32)
    height = (
        jnp.arange(device_list, dtype=jnp.int32)[None, :] * planes
        + jnp.arange(planes, dtype=jnp.int32)[:, None]
    )
    half = (lengths - 1) // 2
    shift_angle = -turning(height.T[:, :, None] * half[None, None, :] % NG)
    shift = (jnp.cos(shift_angle), jnp.sin(shift_angle))
    mask = (order[None, :] < lengths[:, None]).astype(jnp.float32)
    return (shift, mask)


def wave_table():
    angle = 2.0 * np.pi * (np.outer(np.arange(STICK_COEFFS), np.arange(NG)) % NG) / NG
    return ((np.cos(angle) * NG**-0.5).astype(np.float32), (np.sin(angle) * NG**-0.5).astype(np.float32))


def row_layout(device_list):
    half = [math.isqrt(RAD * RAD - (i - RAD) ** 2) for i in range(SIDE)]
    lanes = -(-sum(2 * h + 1 for h in half) // device_list)
    lanes = -(-lanes // LANE) * LANE
    order = sorted(range(SIDE), key=lambda i: (-half[i], i))
    while True:
        used = [0] * device_list
        place = [None] * SIDE
        for i in order:
            device = min(range(device_list), key=lambda d: (used[d], d))
            place[i] = (device, used[device])
            used[device] += 2 * half[i] + 1
        if max(used) <= lanes:
            return half, place, lanes
        lanes += LANE


def height_table(planes, device_list):
    freq = np.arange(KZ) - RAD
    angle = 2.0 * np.pi * (np.outer(np.arange(NG), freq) % NG) / NG
    keep = (np.arange(KZ) < SIDE) * NG**-0.5
    cosine = np.cos(angle) * keep
    sine = np.sin(angle) * keep
    table = np.block([[cosine, -sine], [sine, cosine]]).reshape(2, device_list, planes, 2 * KZ)
    return np.ascontiguousarray(table.transpose(1, 0, 2, 3).reshape(2 * NG, 2 * KZ)).astype(np.float32)


def plane_tables():
    freq = np.arange(KX) - RAD
    angle = 2.0 * np.pi * (np.outer(freq, np.arange(NG)) % NG) / NG
    keep = (np.arange(KX) < SIDE)[:, None] * NG**-0.5
    cosine = np.cos(angle) * keep
    sine = np.sin(angle) * keep
    inner = np.concatenate([cosine, sine], axis=0).T
    outer = np.concatenate([cosine, sine], axis=1)
    lines = np.zeros((LANE, 2, LANE))
    lines[:KY, 0, :NG] = cosine
    lines[:KY, 1, :NG] = sine
    back = np.zeros((2, LANE, 2, LANE))
    back[0, :NG, 0, :KY] = cosine.T
    back[1, :NG, 0, :KY] = sine.T
    back[0, :NG, 1, :KY] = -sine.T
    back[1, :NG, 1, :KY] = cosine.T
    return (
        np.ascontiguousarray(inner).astype(np.float32),
        outer.astype(np.float32),
        lines.reshape(LANE, 2 * LANE).astype(np.float32),
        back.reshape(2 * LANE, 2 * LANE).astype(np.float32),
    )


def thirds(values):
    first = values.astype(jnp.bfloat16).astype(jnp.float32)
    rest = values - first
    second = rest.astype(jnp.bfloat16).astype(jnp.float32)
    return jnp.concatenate([first, second, rest - second], axis=0).astype(jnp.bfloat16)


def add_thirds(parts):
    rows = parts.shape[0] // 3
    return parts[:rows] + parts[rows : 2 * rows] + parts[2 * rows :]


def spread_kernel(cells_ref, values_ref, out_ref):
    groups, rows, lanes = out_ref.shape
    slots = cells_ref.shape[1]
    index = lax.broadcasted_iota(jnp.int32, (slots, groups * lanes), 1)
    hits = jnp.where(index == cells_ref[0], 1.0, 0.0).astype(jnp.bfloat16)

    @pl.when(pl.program_id(0) == 0)
    def _():
        out_ref[...] = jnp.zeros_like(out_ref)

    parts = jnp.dot(thirds(values_ref[0]), hits, preferred_element_type=jnp.float32)
    whole = add_thirds(parts)
    for group in range(groups):
        out_ref[group] += whole[:rows, group * lanes : (group + 1) * lanes]


def pick_kernel(cells_ref, values_ref, out_ref):
    slots = cells_ref.shape[2]
    index = lax.broadcasted_iota(jnp.int32, (values_ref.shape[1], slots), 0)
    hits = jnp.where(index == cells_ref[0], 1.0, 0.0).astype(jnp.bfloat16)
    parts = jnp.dot(thirds(values_ref[...]), hits, preferred_element_type=jnp.float32)
    out_ref[0] = add_thirds(parts)[: out_ref.shape[1]]


def spread(cells, values, groups, lanes):
    sources, rows, slots = values.shape
    padded = -(-rows // 8) * 8
    values = jnp.pad(values, ((0, 0), (0, padded - rows), (0, 0)))
    return pl.pallas_call(
        spread_kernel,
        grid=(sources,),
        in_specs=[
            pl.BlockSpec((1, slots, 1), lambda i: (i, 0, 0)),
            pl.BlockSpec((1, padded, slots), lambda i: (i, 0, 0)),
        ],
        out_specs=pl.BlockSpec((groups, rows, lanes), lambda i: (0, 0, 0)),
        out_shape=jax.ShapeDtypeStruct((groups, rows, lanes), jnp.float32),
        compiler_params=pltpu.CompilerParams(vmem_limit_bytes=40 << 20),
    )(cells[:, :, None], values)


def pick(cells, values):
    sources, slots = cells.shape
    rows, count = values.shape
    padded = -(-rows // 8) * 8
    values = jnp.pad(values, ((0, padded - rows), (0, 0)))
    return pl.pallas_call(
        pick_kernel,
        grid=(sources,),
        in_specs=[
            pl.BlockSpec((1, 1, slots), lambda i: (i, 0, 0)),
            pl.BlockSpec((padded, count), lambda i: (0, 0)),
        ],
        out_specs=pl.BlockSpec((1, rows, slots), lambda i: (i, 0, 0)),
        out_shape=jax.ShapeDtypeStruct((sources, rows, slots), jnp.float32),
        compiler_params=pltpu.CompilerParams(vmem_limit_bytes=40 << 20),
    )(cells[:, None, :], values)


def product(left, right):
    return jnp.dot(left, right, precision=HIGHEST, preferred_element_type=jnp.float32)


def halves(values):
    first = values.astype(jnp.bfloat16)
    return first, (values - first.astype(jnp.float32)).astype(jnp.bfloat16)


def product_halves(left, right):
    def one(a, b):
        return jnp.dot(a, b, preferred_element_type=jnp.float32)

    return one(left[0], right[0]) + (one(left[0], right[1]) + one(left[1], right[0]))


def plane_kernel(layout, pitch, with_modulus, with_back, *refs):
    half, place, _ = layout
    arrived_ref, local_ref, inner_ref, outer_ref, lines_ref, back_ref = refs[:6]
    refs = refs[6:]
    if with_back:
        out_ref, refs = refs[0], refs[1:]
    if with_modulus:
        modulus_ref, refs = refs[0], refs[1:]
    box, cosine_part, sine_part = refs
    planes = local_ref.shape[0]
    rows = 2 * planes
    box[...] = jnp.zeros_like(box)
    for i in range(SIDE):
        device, lane = place[i]
        width = 2 * half[i] + 1
        box[i * pitch : i * pitch + rows, RAD - half[i] : RAD + half[i] + 1] = arrived_ref[
            device, :, lane : lane + width
        ]
    inner, outer = halves(inner_ref[...]), halves(outer_ref[...])
    turned = product_halves(halves(box[...]), halves(lines_ref[...]))
    cosine_part[...] = turned[:, :LANE]
    sine_part[...] = turned[:, LANE:]
    group = max(size for size in range(1, 5) if planes % size == 0)
    for begin in range(0, planes, group):
        top, bottom = [], []
        for p in range(begin, begin + group):
            real = pl.ds(p, KX, stride=pitch)
            imag = pl.ds(planes + p, KX, stride=pitch)
            line_real = cosine_part[real, :] - sine_part[imag, :]
            line_imag = sine_part[real, :] + cosine_part[imag, :]
            top += [line_real, line_imag]
            bottom += [-line_imag, line_real]
        lines = jnp.concatenate(
            [jnp.concatenate(top, axis=1), jnp.concatenate(bottom, axis=1)], axis=0
        )
        field = product_halves(inner, halves(lines))
        top, bottom = [], []
        for q in range(group):
            p = begin + q
            field_real = field[:, 2 * q * LANE : (2 * q + 1) * LANE]
            field_imag = field[:, (2 * q + 1) * LANE : (2 * q + 2) * LANE]
            if with_modulus:
                modulus_ref[p] = field_real * field_real + field_imag * field_imag
            if with_back:
                field_real = field_real * local_ref[p]
                field_imag = field_imag * local_ref[p]
                top += [field_real, field_imag]
                bottom += [field_imag, -field_real]
        if with_back:
            both = jnp.concatenate(
                [jnp.concatenate(top, axis=1), jnp.concatenate(bottom, axis=1)], axis=0
            )
            result = product_halves(outer, halves(both))
            result = jnp.concatenate(
                [result[:, 2 * q * LANE : (2 * q + 2) * LANE] for q in range(group)], axis=0
            )
            result = product_halves(halves(result), halves(back_ref[...]))
            for q in range(group):
                p = begin + q
                part = result[q * KX : (q + 1) * KX]
                box[pl.ds(p, KX, stride=pitch), :] = part[:, :LANE]
                box[pl.ds(planes + p, KX, stride=pitch), :] = part[:, LANE:]
    if with_back:
        out_ref[...] = jnp.zeros_like(out_ref)
        for i in range(SIDE):
            device, lane = place[i]
            width = 2 * half[i] + 1
            out_ref[device, :, lane : lane + width] = box[
                i * pitch : i * pitch + rows, RAD - half[i] : RAD + half[i] + 1
            ]


def plane_step(layout, arrived, local, tables, with_modulus, with_back):
    planes = local.shape[0]
    pitch = -(-2 * planes // 8) * 8
    shapes = []
    if with_back:
        shapes.append(jax.ShapeDtypeStruct(arrived.shape, jnp.float32))
    if with_modulus:
        shapes.append(jax.ShapeDtypeStruct(local.shape, jnp.float32))
    kernel = functools.partial(plane_kernel, layout, pitch, with_modulus, with_back)
    whole = pl.BlockSpec(memory_space=pltpu.VMEM)
    return pl.pallas_call(
        kernel,
        in_specs=[whole] * 6,
        out_specs=[whole] * len(shapes),
        out_shape=shapes,
        scratch_shapes=[pltpu.VMEM((KX * pitch, LANE), jnp.float32)] * 3,
        compiler_params=pltpu.CompilerParams(vmem_limit_bytes=40 << 20),
    )(arrived, local, *tables)


def trade(count, sent, landed, send_sem, recv_sem):
    me = lax.axis_index("plane")
    band = lax.axis_index("band")
    copies = []
    for k in range(1, count):
        partner = lax.rem(me + k, count)
        copy = pltpu.make_async_remote_copy(
            src_ref=sent.at[partner],
            dst_ref=landed.at[me],
            send_sem=send_sem.at[k - 1],
            recv_sem=recv_sem.at[k - 1],
            device_id=(band, partner),
            device_id_type=pl.DeviceIdType.MESH,
        )
        copy.start()
        copies.append(copy)
    landed[me] = sent[me]
    return copies


def height_kernel(count, factor, opening, last, *refs):
    spectrum_ref, term_ref, total_ref, kinetic_ref, inside_ref, table_ref, turned_ref = refs[:7]
    outs, scratch = refs[7 : 8 if last else 10], refs[8 if last else 10 :]
    landed, sent, final, flat, send_sem, recv_sem, send_later, recv_later = scratch[:8]
    me = lax.axis_index("plane")
    band = lax.axis_index("band")
    barrier = pltpu.get_barrier_semaphore()
    for k in range(1, count):
        pl.semaphore_signal(
            barrier,
            inc=1,
            device_id=(band, lax.rem(me + k, count)),
            device_id_type=pl.DeviceIdType.MESH,
        )
    pl.semaphore_wait(barrier, count - 1)
    copies = trade(count, spectrum_ref, landed, send_sem, recv_sem)
    if opening:
        origin, origin_send, origin_recv = scratch[8:]
        copies += trade(count, term_ref, origin, origin_send, origin_recv)
    for copy in copies:
        copy.wait()
    rows = landed.shape[1]
    table, turned, inside = table_ref[...], turned_ref[...], inside_ref[...]

    def gathered(buffer):
        for d in range(count):
            flat[d * rows : (d + 1) * rows, :] = buffer[d]
        return product(turned, flat[...]) * inside

    before = gathered(origin) if opening else term_ref[...]
    total = before if opening else total_ref[...]
    applied = gathered(landed) + kinetic_ref[...] * before
    term = factor * jnp.concatenate([applied[KZ:], -applied[:KZ]], axis=0)
    total = total + term
    flat[...] = product(table, total if last else term)
    for d in range(count):
        sent[d] = flat[d * rows : (d + 1) * rows, :]
    copies = trade(count, sent, final, send_later, recv_later)
    if not last:
        outs[1][...] = term
        outs[2][...] = total
    for copy in copies:
        copy.wait()
    outs[0][...] = final[...]


def height_step(power, spectrum, term, total, kinetic, inside, table):
    count, rows, lanes = spectrum.shape
    opening, last = power == 1, power == 3
    shapes = [jax.ShapeDtypeStruct(spectrum.shape, jnp.float32)]
    if not last:
        shapes += [jax.ShapeDtypeStruct((table.shape[1], lanes), jnp.float32)] * 2
    whole = pl.BlockSpec(memory_space=pltpu.VMEM)
    block = pltpu.VMEM((count, rows, lanes), jnp.float32)
    marks = pltpu.SemaphoreType.DMA((count - 1,))
    return pl.pallas_call(
        functools.partial(height_kernel, count, TIMESTEP / power, opening, last),
        in_specs=[whole] * 7,
        out_specs=[whole] * len(shapes),
        out_shape=shapes,
        scratch_shapes=[block] * 3
        + [pltpu.VMEM((count * rows, lanes), jnp.float32)]
        + [marks] * 4
        + ([block, marks, marks] if opening else []),
        compiler_params=pltpu.CompilerParams(
            vmem_limit_bytes=40 << 20, collective_id=power, has_side_effects=True
        ),
    )(spectrum, term, total, kinetic, inside, table, np.ascontiguousarray(table.T))


def dot(subscripts, left, right):
    return jnp.einsum(subscripts, left, right, precision=HIGHEST)


def sum_bands(values):
    bands = lax.axis_size("band")
    if bands & (bands - 1):
        return lax.psum(values, "band")
    step = 1
    while step < bands:
        pairs = [(i, i ^ step) for i in range(bands)]
        values = values + lax.ppermute(values, "band", pairs)
        step *= 2
    return values


def shards(psi, potential, stick_column, stick_length):
    device_list = lax.axis_size("plane")
    planes = potential.shape[0]
    slots = stick_column.shape[0]
    layout = row_layout(device_list)
    half, place, lanes = layout
    wave = wave_table()
    shift, mask = height_tables(stick_length, planes, device_list)

    def exchange(values):
        return lax.all_to_all(values, "plane", split_axis=0, concat_axis=0, tiled=True)

    term = psi[:, 0] * mask
    upper = [
        dot("sj,jz->zs", term[0], wave[0]) - dot("sj,jz->zs", term[1], wave[1]),
        dot("sj,jz->zs", term[0], wave[1]) + dot("sj,jz->zs", term[1], wave[0]),
    ]
    upper = [part.reshape(device_list, planes, slots) for part in upper]
    first = signed(stick_column // NG)
    second = signed(stick_column % NG)
    base = np.array([place[i][0] * lanes + place[i][1] + half[i] for i in range(SIDE)], np.int32)
    chosen = first[None, :] + RAD == jnp.arange(SIDE, dtype=jnp.int32)[:, None]
    own_cell = jnp.sum(jnp.where(chosen, base[:, None], 0), axis=0) + second
    own_cell = jnp.where(stick_length > 0, own_cell, -1)
    packed = jnp.concatenate(
        [
            upper[0] * shift[0] - upper[1] * shift[1],
            upper[0] * shift[1] + upper[1] * shift[0],
            jnp.broadcast_to(own_cell.astype(jnp.float32), (device_list, 1, slots)),
        ],
        axis=1,
    )
    arrived = exchange(packed)
    cells = arrived[:, 2 * planes, :].astype(jnp.int32)
    start = spread(cells, arrived[:, : 2 * planes, :], device_list, lanes)

    local = jnp.pad(potential.reshape(planes, NG, NG), ((0, 0), (0, 0), (0, LANE - NG)))
    tables = plane_tables()
    table = height_table(planes, device_list)
    planar = np.full((device_list, lanes), 4 * RAD * RAD, np.int32)
    for i in range(SIDE):
        device, lane = place[i]
        spot = np.arange(-half[i], half[i] + 1)
        planar[device, lane : lane + 2 * half[i] + 1] = (i - RAD) ** 2 + spot * spot
    planar = lax.dynamic_slice_in_dim(jnp.asarray(planar), lax.axis_index("plane"), 1, 0)
    depth = np.concatenate([np.arange(KZ) - RAD] * 2).astype(np.int32)[:, None]
    square = planar + depth * depth
    inside = (square <= RAD * RAD).astype(jnp.float32)
    kinetic = square.astype(jnp.float32) / (RAD * RAD) * inside

    spectrum, before = plane_step(layout, start, local, tables, True, True)
    arrived, term, total = height_step(1, spectrum, start, kinetic, kinetic, inside, table)
    (spectrum,) = plane_step(layout, arrived, local, tables, False, True)
    arrived, term, total = height_step(2, spectrum, term, total, kinetic, inside, table)
    (spectrum,) = plane_step(layout, arrived, local, tables, False, True)
    (final,) = height_step(3, spectrum, term, total, kinetic, inside, table)
    (after,) = plane_step(layout, final, local, tables, True, False)
    flat = final.transpose(1, 0, 2).reshape(2 * planes, device_list * lanes)
    home = exchange(pick(cells, flat))
    real, imag = home[:, :planes], home[:, planes:]
    turned = [
        (real * shift[0] + imag * shift[1]).reshape(NG, slots),
        (imag * shift[0] - real * shift[1]).reshape(NG, slots),
    ]
    psi_new = jnp.stack(
        [
            (dot("zs,jz->sj", turned[0], wave[0]) + dot("zs,jz->sj", turned[1], wave[1])) * mask,
            (dot("zs,jz->sj", turned[1], wave[0]) - dot("zs,jz->sj", turned[0], wave[1])) * mask,
        ]
    )[:, None]
    change = (after - before)[..., :NG].reshape(planes, NG * NG) / BAND_DEV
    whole = sum_bands(change)
    potential_new = potential + LINEAR_GAIN * whole + CUBIC_GAIN * whole * whole * whole
    return (psi_new, potential_new)


def solution(mesh):
    in_specs = (P(None, "band", "plane", None), P("plane", None), P("plane"), P("plane"))
    out_specs = (P(None, "band", "plane", None), P("plane", None))
    return jax.shard_map(shards, mesh=mesh, in_specs=in_specs, out_specs=out_specs, check_vma=False)
```

```python
import functools
import math

import jax
import jax.numpy as jnp
import numpy as np
from jax import lax
from jax.experimental import pallas as pl
from jax.experimental.pallas import tpu as pltpu
from jax.sharding import PartitionSpec as P

NG = 96
RAD = 24
STICK_COEFFS = 128
BAND_DEV = 1
SIDE = 2 * RAD + 1
KY = 64
KX = 64
KZ = 56
LANE = 128

HIGHEST = lax.Precision.HIGHEST
TIMESTEP = 0.6
LINEAR_GAIN = 0.5
CUBIC_GAIN = 0.3


def turning(values):
    return values.astype(jnp.float32) * (2.0 * math.pi / NG)


def signed(index):
    return jnp.where(index > NG // 2, index - NG, index)


def height_tables(lengths, planes, device_list):
    order = jnp.arange(STICK_COEFFS, dtype=jnp.int32)
    height = (
        jnp.arange(device_list, dtype=jnp.int32)[None, :] * planes
        + jnp.arange(planes, dtype=jnp.int32)[:, None]
    )
    half = (lengths - 1) // 2
    shift_angle = -turning(height.T[:, :, None] * half[None, None, :] % NG)
    shift = (jnp.cos(shift_angle), jnp.sin(shift_angle))
    mask = (order[None, :] < lengths[:, None]).astype(jnp.float32)
    return (shift, mask)


def wave_table():
    angle = 2.0 * np.pi * (np.outer(np.arange(STICK_COEFFS), np.arange(NG)) % NG) / NG
    return ((np.cos(angle) * NG**-0.5).astype(np.float32), (np.sin(angle) * NG**-0.5).astype(np.float32))


def row_layout(device_list):
    half = [math.isqrt(RAD * RAD - (i - RAD) ** 2) for i in range(SIDE)]
    lanes = -(-sum(2 * h + 1 for h in half) // device_list)
    lanes = -(-lanes // LANE) * LANE
    order = sorted(range(SIDE), key=lambda i: (-half[i], i))
    while True:
        used = [0] * device_list
        place = [None] * SIDE
        for i in order:
            device = min(range(device_list), key=lambda d: (used[d], d))
            place[i] = (device, used[device])
            used[device] += 2 * half[i] + 1
        if max(used) <= lanes:
            return half, place, lanes
        lanes += LANE


def height_table(planes, device_list):
    freq = np.arange(KZ) - RAD
    angle = 2.0 * np.pi * (np.outer(np.arange(NG), freq) % NG) / NG
    keep = (np.arange(KZ) < SIDE) * NG**-0.5
    cosine = np.cos(angle) * keep
    sine = np.sin(angle) * keep
    table = np.block([[cosine, -sine], [sine, cosine]]).reshape(2, device_list, planes, 2 * KZ)
    return np.ascontiguousarray(table.transpose(1, 0, 2, 3).reshape(2 * NG, 2 * KZ)).astype(np.float32)


def plane_tables():
    freq = np.arange(KX) - RAD
    angle = 2.0 * np.pi * (np.outer(freq, np.arange(NG)) % NG) / NG
    keep = (np.arange(KX) < SIDE)[:, None] * NG**-0.5
    cosine = np.cos(angle) * keep
    sine = np.sin(angle) * keep
    inner = np.concatenate([cosine, sine], axis=0).T
    outer = np.concatenate([cosine, sine], axis=1)
    lines = np.zeros((LANE, 2, LANE))
    lines[:KY, 0, :NG] = cosine
    lines[:KY, 1, :NG] = sine
    back = np.zeros((2, LANE, 2, LANE))
    back[0, :NG, 0, :KY] = cosine.T
    back[1, :NG, 0, :KY] = sine.T
    back[0, :NG, 1, :KY] = -sine.T
    back[1, :NG, 1, :KY] = cosine.T
    return (
        np.ascontiguousarray(inner).astype(np.float32),
        outer.astype(np.float32),
        lines.reshape(LANE, 2 * LANE).astype(np.float32),
        back.reshape(2 * LANE, 2 * LANE).astype(np.float32),
    )


def thirds(values):
    first = values.astype(jnp.bfloat16).astype(jnp.float32)
    rest = values - first
    second = rest.astype(jnp.bfloat16).astype(jnp.float32)
    return jnp.concatenate([first, second, rest - second], axis=0).astype(jnp.bfloat16)


def add_thirds(parts):
    rows = parts.shape[0] // 3
    return parts[:rows] + parts[rows : 2 * rows] + parts[2 * rows :]


def spread_kernel(cells_ref, values_ref, out_ref):
    groups, rows, lanes = out_ref.shape
    slots = cells_ref.shape[1]
    index = lax.broadcasted_iota(jnp.int32, (slots, groups * lanes), 1)
    hits = jnp.where(index == cells_ref[0], 1.0, 0.0).astype(jnp.bfloat16)

    @pl.when(pl.program_id(0) == 0)
    def _():
        out_ref[...] = jnp.zeros_like(out_ref)

    parts = jnp.dot(thirds(values_ref[0]), hits, preferred_element_type=jnp.float32)
    whole = add_thirds(parts)
    for group in range(groups):
        out_ref[group] += whole[:rows, group * lanes : (group + 1) * lanes]


def pick_kernel(cells_ref, values_ref, out_ref):
    slots = cells_ref.shape[2]
    index = lax.broadcasted_iota(jnp.int32, (values_ref.shape[1], slots), 0)
    hits = jnp.where(index == cells_ref[0], 1.0, 0.0).astype(jnp.bfloat16)
    parts = jnp.dot(thirds(values_ref[...]), hits, preferred_element_type=jnp.float32)
    out_ref[0] = add_thirds(parts)[: out_ref.shape[1]]


def spread(cells, values, groups, lanes):
    sources, rows, slots = values.shape
    padded = -(-rows // 8) * 8
    values = jnp.pad(values, ((0, 0), (0, padded - rows), (0, 0)))
    return pl.pallas_call(
        spread_kernel,
        grid=(sources,),
        in_specs=[
            pl.BlockSpec((1, slots, 1), lambda i: (i, 0, 0)),
            pl.BlockSpec((1, padded, slots), lambda i: (i, 0, 0)),
        ],
        out_specs=pl.BlockSpec((groups, rows, lanes), lambda i: (0, 0, 0)),
        out_shape=jax.ShapeDtypeStruct((groups, rows, lanes), jnp.float32),
        compiler_params=pltpu.CompilerParams(vmem_limit_bytes=40 << 20),
    )(cells[:, :, None], values)


def pick(cells, values):
    sources, slots = cells.shape
    rows, count = values.shape
    padded = -(-rows // 8) * 8
    values = jnp.pad(values, ((0, padded - rows), (0, 0)))
    return pl.pallas_call(
        pick_kernel,
        grid=(sources,),
        in_specs=[
            pl.BlockSpec((1, 1, slots), lambda i: (i, 0, 0)),
            pl.BlockSpec((padded, count), lambda i: (0, 0)),
        ],
        out_specs=pl.BlockSpec((1, rows, slots), lambda i: (i, 0, 0)),
        out_shape=jax.ShapeDtypeStruct((sources, rows, slots), jnp.float32),
        compiler_params=pltpu.CompilerParams(vmem_limit_bytes=40 << 20),
    )(cells[:, None, :], values)


def product(left, right):
    return jnp.dot(left, right, precision=HIGHEST, preferred_element_type=jnp.float32)


def halves(values):
    first = values.astype(jnp.bfloat16)
    return first, (values - first.astype(jnp.float32)).astype(jnp.bfloat16)


def product_halves(left, right):
    def one(a, b):
        return jnp.dot(a, b, preferred_element_type=jnp.float32)

    return one(left[0], right[0]) + (one(left[0], right[1]) + one(left[1], right[0]))


def plane_kernel(layout, pitch, with_modulus, with_back, *refs):
    half, place, _ = layout
    arrived_ref, local_ref, inner_ref, outer_ref, lines_ref, back_ref = refs[:6]
    refs = refs[6:]
    if with_back:
        out_ref, refs = refs[0], refs[1:]
    if with_modulus:
        modulus_ref, refs = refs[0], refs[1:]
    box, cosine_part, sine_part = refs
    planes = local_ref.shape[0]
    rows = 2 * planes
    box[...] = jnp.zeros_like(box)
    for i in range(SIDE):
        device, lane = place[i]
        width = 2 * half[i] + 1
        box[i * pitch : i * pitch + rows, RAD - half[i] : RAD + half[i] + 1] = arrived_ref[
            device, :, lane : lane + width
        ]
    inner, outer = halves(inner_ref[...]), halves(outer_ref[...])
    turned = product_halves(halves(box[...]), halves(lines_ref[...]))
    cosine_part[...] = turned[:, :LANE]
    sine_part[...] = turned[:, LANE:]
    group = max(size for size in range(1, 5) if planes % size == 0)
    for begin in range(0, planes, group):
        top, bottom = [], []
        for p in range(begin, begin + group):
            real = pl.ds(p, KX, stride=pitch)
            imag = pl.ds(planes + p, KX, stride=pitch)
            line_real = cosine_part[real, :] - sine_part[imag, :]
            line_imag = sine_part[real, :] + cosine_part[imag, :]
            top += [line_real, line_imag]
            bottom += [-line_imag, line_real]
        lines = jnp.concatenate(
            [jnp.concatenate(top, axis=1), jnp.concatenate(bottom, axis=1)], axis=0
        )
        field = product_halves(inner, halves(lines))
        top, bottom = [], []
        for q in range(group):
            p = begin + q
            field_real = field[:, 2 * q * LANE : (2 * q + 1) * LANE]
            field_imag = field[:, (2 * q + 1) * LANE : (2 * q + 2) * LANE]
            if with_modulus:
                modulus_ref[p] = field_real * field_real + field_imag * field_imag
            if with_back:
                field_real = field_real * local_ref[p]
                field_imag = field_imag * local_ref[p]
                top += [field_real, field_imag]
                bottom += [field_imag, -field_real]
        if with_back:
            both = jnp.concatenate(
                [jnp.concatenate(top, axis=1), jnp.concatenate(bottom, axis=1)], axis=0
            )
            result = product_halves(outer, halves(both))
            result = jnp.concatenate(
                [result[:, 2 * q * LANE : (2 * q + 2) * LANE] for q in range(group)], axis=0
            )
            result = product_halves(halves(result), halves(back_ref[...]))
            for q in range(group):
                p = begin + q
                part = result[q * KX : (q + 1) * KX]
                box[pl.ds(p, KX, stride=pitch), :] = part[:, :LANE]
                box[pl.ds(planes + p, KX, stride=pitch), :] = part[:, LANE:]
    if with_back:
        out_ref[...] = jnp.zeros_like(out_ref)
        for i in range(SIDE):
            device, lane = place[i]
            width = 2 * half[i] + 1
            out_ref[device, :, lane : lane + width] = box[
                i * pitch : i * pitch + rows, RAD - half[i] : RAD + half[i] + 1
            ]


def plane_step(layout, arrived, local, tables, with_modulus, with_back):
    planes = local.shape[0]
    pitch = -(-2 * planes // 8) * 8
    shapes = []
    if with_back:
        shapes.append(jax.ShapeDtypeStruct(arrived.shape, jnp.float32))
    if with_modulus:
        shapes.append(jax.ShapeDtypeStruct(local.shape, jnp.float32))
    kernel = functools.partial(plane_kernel, layout, pitch, with_modulus, with_back)
    whole = pl.BlockSpec(memory_space=pltpu.VMEM)
    return pl.pallas_call(
        kernel,
        in_specs=[whole] * 6,
        out_specs=[whole] * len(shapes),
        out_shape=shapes,
        scratch_shapes=[pltpu.VMEM((KX * pitch, LANE), jnp.float32)] * 3,
        compiler_params=pltpu.CompilerParams(vmem_limit_bytes=40 << 20),
    )(arrived, local, *tables)


def trade(count, sent, landed, send_sem, recv_sem):
    me = lax.axis_index("plane")
    band = lax.axis_index("band")
    copies = []
    for k in range(1, count):
        partner = lax.rem(me + k, count)
        copy = pltpu.make_async_remote_copy(
            src_ref=sent.at[partner],
            dst_ref=landed.at[me],
            send_sem=send_sem.at[k - 1],
            recv_sem=recv_sem.at[k - 1],
            device_id=(band, partner),
            device_id_type=pl.DeviceIdType.MESH,
        )
        copy.start()
        copies.append(copy)
    landed[me] = sent[me]
    return copies


def greet(count):
    me = lax.axis_index("plane")
    band = lax.axis_index("band")
    barrier = pltpu.get_barrier_semaphore()
    for k in range(1, count):
        pl.semaphore_signal(
            barrier,
            inc=1,
            device_id=(band, lax.rem(me + k, count)),
            device_id_type=pl.DeviceIdType.MESH,
        )
    pl.semaphore_wait(barrier, count - 1)


def swap_kernel(count, sent_ref, out_ref, landed, send_sem, recv_sem):
    greet(count)
    for copy in trade(count, sent_ref, landed, send_sem, recv_sem):
        copy.wait()
    out_ref[...] = landed[...]


def swap(values, collective_id):
    count = values.shape[0]
    whole = pl.BlockSpec(memory_space=pltpu.VMEM)
    return pl.pallas_call(
        functools.partial(swap_kernel, count),
        in_specs=[whole],
        out_specs=whole,
        out_shape=jax.ShapeDtypeStruct(values.shape, jnp.float32),
        scratch_shapes=[pltpu.VMEM(values.shape, jnp.float32)]
        + [pltpu.SemaphoreType.DMA((count - 1,))] * 2,
        compiler_params=pltpu.CompilerParams(
            vmem_limit_bytes=40 << 20, collective_id=collective_id, has_side_effects=True
        ),
    )(values)


def height_kernel(count, factor, opening, last, *refs):
    spectrum_ref, term_ref, total_ref, kinetic_ref, inside_ref, table_ref, turned_ref = refs[:7]
    outs, scratch = refs[7 : 8 if last else 10], refs[8 if last else 10 :]
    landed, sent, final, flat, send_sem, recv_sem, send_later, recv_later = scratch[:8]
    greet(count)
    copies = trade(count, spectrum_ref, landed, send_sem, recv_sem)
    if opening:
        origin, origin_send, origin_recv = scratch[8:]
        copies += trade(count, term_ref, origin, origin_send, origin_recv)
    for copy in copies:
        copy.wait()
    rows = landed.shape[1]
    table, turned, inside = table_ref[...], turned_ref[...], inside_ref[...]

    def gathered(buffer):
        for d in range(count):
            flat[d * rows : (d + 1) * rows, :] = buffer[d]
        return product(turned, flat[...]) * inside

    before = gathered(origin) if opening else term_ref[...]
    total = before if opening else total_ref[...]
    applied = gathered(landed) + kinetic_ref[...] * before
    term = factor * jnp.concatenate([applied[KZ:], -applied[:KZ]], axis=0)
    total = total + term
    flat[...] = product(table, total if last else term)
    for d in range(count):
        sent[d] = flat[d * rows : (d + 1) * rows, :]
    copies = trade(count, sent, final, send_later, recv_later)
    if not last:
        outs[1][...] = term
        outs[2][...] = total
    for copy in copies:
        copy.wait()
    outs[0][...] = final[...]


def height_step(power, spectrum, term, total, kinetic, inside, table):
    count, rows, lanes = spectrum.shape
    opening, last = power == 1, power == 3
    shapes = [jax.ShapeDtypeStruct(spectrum.shape, jnp.float32)]
    if not last:
        shapes += [jax.ShapeDtypeStruct((table.shape[1], lanes), jnp.float32)] * 2
    whole = pl.BlockSpec(memory_space=pltpu.VMEM)
    block = pltpu.VMEM((count, rows, lanes), jnp.float32)
    marks = pltpu.SemaphoreType.DMA((count - 1,))
    return pl.pallas_call(
        functools.partial(height_kernel, count, TIMESTEP / power, opening, last),
        in_specs=[whole] * 7,
        out_specs=[whole] * len(shapes),
        out_shape=shapes,
        scratch_shapes=[block] * 3
        + [pltpu.VMEM((count * rows, lanes), jnp.float32)]
        + [marks] * 4
        + ([block, marks, marks] if opening else []),
        compiler_params=pltpu.CompilerParams(
            vmem_limit_bytes=40 << 20, collective_id=power, has_side_effects=True
        ),
    )(spectrum, term, total, kinetic, inside, table, np.ascontiguousarray(table.T))


def dot(subscripts, left, right):
    return jnp.einsum(subscripts, left, right, precision=HIGHEST)


def sum_bands(values):
    bands = lax.axis_size("band")
    if bands & (bands - 1):
        return lax.psum(values, "band")
    step = 1
    while step < bands:
        pairs = [(i, i ^ step) for i in range(bands)]
        values = values + lax.ppermute(values, "band", pairs)
        step *= 2
    return values


def shards(psi, potential, stick_column, stick_length):
    device_list = lax.axis_size("plane")
    planes = potential.shape[0]
    slots = stick_column.shape[0]
    layout = row_layout(device_list)
    half, place, lanes = layout
    wave = wave_table()
    shift, mask = height_tables(stick_length, planes, device_list)

    def exchange(values):
        return lax.all_to_all(values, "plane", split_axis=0, concat_axis=0, tiled=True)

    term = psi[:, 0] * mask
    upper = [
        dot("sj,jz->zs", term[0], wave[0]) - dot("sj,jz->zs", term[1], wave[1]),
        dot("sj,jz->zs", term[0], wave[1]) + dot("sj,jz->zs", term[1], wave[0]),
    ]
    upper = [part.reshape(device_list, planes, slots) for part in upper]
    first = signed(stick_column // NG)
    second = signed(stick_column % NG)
    base = np.array([place[i][0] * lanes + place[i][1] + half[i] for i in range(SIDE)], np.int32)
    chosen = first[None, :] + RAD == jnp.arange(SIDE, dtype=jnp.int32)[:, None]
    own_cell = jnp.sum(jnp.where(chosen, base[:, None], 0), axis=0) + second
    own_cell = jnp.where(stick_length > 0, own_cell, -1)
    packed = jnp.concatenate(
        [
            upper[0] * shift[0] - upper[1] * shift[1],
            upper[0] * shift[1] + upper[1] * shift[0],
            jnp.broadcast_to(own_cell.astype(jnp.float32), (device_list, 1, slots)),
        ],
        axis=1,
    )
    arrived = swap(packed, 4)
    cells = arrived[:, 2 * planes, :].astype(jnp.int32)
    start = spread(cells, arrived[:, : 2 * planes, :], device_list, lanes)

    local = jnp.pad(potential.reshape(planes, NG, NG), ((0, 0), (0, 0), (0, LANE - NG)))
    tables = plane_tables()
    table = height_table(planes, device_list)
    planar = np.full((device_list, lanes), 4 * RAD * RAD, np.int32)
    for i in range(SIDE):
        device, lane = place[i]
        spot = np.arange(-half[i], half[i] + 1)
        planar[device, lane : lane + 2 * half[i] + 1] = (i - RAD) ** 2 + spot * spot
    planar = lax.dynamic_slice_in_dim(jnp.asarray(planar), lax.axis_index("plane"), 1, 0)
    depth = np.concatenate([np.arange(KZ) - RAD] * 2).astype(np.int32)[:, None]
    square = planar + depth * depth
    inside = (square <= RAD * RAD).astype(jnp.float32)
    kinetic = square.astype(jnp.float32) / (RAD * RAD) * inside

    spectrum, before = plane_step(layout, start, local, tables, True, True)
    arrived, term, total = height_step(1, spectrum, start, kinetic, kinetic, inside, table)
    (spectrum,) = plane_step(layout, arrived, local, tables, False, True)
    arrived, term, total = height_step(2, spectrum, term, total, kinetic, inside, table)
    (spectrum,) = plane_step(layout, arrived, local, tables, False, True)
    (final,) = height_step(3, spectrum, term, total, kinetic, inside, table)
    (after,) = plane_step(layout, final, local, tables, True, False)
    flat = final.transpose(1, 0, 2).reshape(2 * planes, device_list * lanes)
    home = exchange(pick(cells, flat))
    real, imag = home[:, :planes], home[:, planes:]
    turned = [
        (real * shift[0] + imag * shift[1]).reshape(NG, slots),
        (imag * shift[0] - real * shift[1]).reshape(NG, slots),
    ]
    psi_new = jnp.stack(
        [
            (dot("zs,jz->sj", turned[0], wave[0]) + dot("zs,jz->sj", turned[1], wave[1])) * mask,
            (dot("zs,jz->sj", turned[1], wave[0]) - dot("zs,jz->sj", turned[0], wave[1])) * mask,
        ]
    )[:, None]
    change = (after - before)[..., :NG].reshape(planes, NG * NG) / BAND_DEV
    whole = sum_bands(change)
    potential_new = potential + LINEAR_GAIN * whole + CUBIC_GAIN * whole * whole * whole
    return (psi_new, potential_new)


def solution(mesh):
    in_specs = (P(None, "band", "plane", None), P("plane", None), P("plane"), P("plane"))
    out_specs = (P(None, "band", "plane", None), P("plane", None))
    return jax.shard_map(shards, mesh=mesh, in_specs=in_specs, out_specs=out_specs, check_vma=False)
```

```python
import functools
import math

import jax
import jax.numpy as jnp
import numpy as np
from jax import lax
from jax.experimental import pallas as pl
from jax.experimental.pallas import tpu as pltpu
from jax.sharding import PartitionSpec as P

NG = 96
RAD = 24
STICK_COEFFS = 128
BAND_DEV = 1
SIDE = 2 * RAD + 1
KY = 64
KX = 64
KZ = 56
LANE = 128

HIGHEST = lax.Precision.HIGHEST
TIMESTEP = 0.6
LINEAR_GAIN = 0.5
CUBIC_GAIN = 0.3


def turning(values):
    return values.astype(jnp.float32) * (2.0 * math.pi / NG)


def signed(index):
    return jnp.where(index > NG // 2, index - NG, index)


def height_tables(lengths, planes, device_list):
    order = jnp.arange(STICK_COEFFS, dtype=jnp.int32)
    height = (
        jnp.arange(device_list, dtype=jnp.int32)[None, :] * planes
        + jnp.arange(planes, dtype=jnp.int32)[:, None]
    )
    half = (lengths - 1) // 2
    shift_angle = -turning(height.T[:, :, None] * half[None, None, :] % NG)
    shift = (jnp.cos(shift_angle), jnp.sin(shift_angle))
    mask = (order[None, :] < lengths[:, None]).astype(jnp.float32)
    return (shift, mask)


def wave_table():
    angle = 2.0 * np.pi * (np.outer(np.arange(STICK_COEFFS), np.arange(NG)) % NG) / NG
    return ((np.cos(angle) * NG**-0.5).astype(np.float32), (np.sin(angle) * NG**-0.5).astype(np.float32))


def row_layout(device_list):
    half = [math.isqrt(RAD * RAD - (i - RAD) ** 2) for i in range(SIDE)]
    lanes = -(-sum(2 * h + 1 for h in half) // device_list)
    lanes = -(-lanes // LANE) * LANE
    order = sorted(range(SIDE), key=lambda i: (-half[i], i))
    while True:
        used = [0] * device_list
        place = [None] * SIDE
        for i in order:
            device = min(range(device_list), key=lambda d: (used[d], d))
            place[i] = (device, used[device])
            used[device] += 2 * half[i] + 1
        if max(used) <= lanes:
            return half, place, lanes
        lanes += LANE


def height_table(planes, device_list):
    freq = np.arange(KZ) - RAD
    angle = 2.0 * np.pi * (np.outer(np.arange(NG), freq) % NG) / NG
    keep = (np.arange(KZ) < SIDE) * NG**-0.5
    cosine = np.cos(angle) * keep
    sine = np.sin(angle) * keep
    table = np.block([[cosine, -sine], [sine, cosine]]).reshape(2, device_list, planes, 2 * KZ)
    return np.ascontiguousarray(table.transpose(1, 0, 2, 3).reshape(2 * NG, 2 * KZ)).astype(np.float32)


def plane_tables():
    freq = np.arange(KX) - RAD
    angle = 2.0 * np.pi * (np.outer(freq, np.arange(NG)) % NG) / NG
    keep = (np.arange(KX) < SIDE)[:, None] * NG**-0.5
    cosine = np.cos(angle) * keep
    sine = np.sin(angle) * keep
    inner = np.concatenate([cosine, sine], axis=0).T
    outer = np.concatenate([cosine, sine], axis=1)
    lines = np.zeros((LANE, 2, LANE))
    lines[:KY, 0, :NG] = cosine
    lines[:KY, 1, :NG] = sine
    back = np.zeros((2, LANE, 2, LANE))
    back[0, :NG, 0, :KY] = cosine.T
    back[1, :NG, 0, :KY] = sine.T
    back[0, :NG, 1, :KY] = -sine.T
    back[1, :NG, 1, :KY] = cosine.T
    return (
        np.ascontiguousarray(inner).astype(np.float32),
        outer.astype(np.float32),
        lines.reshape(LANE, 2 * LANE).astype(np.float32),
        back.reshape(2 * LANE, 2 * LANE).astype(np.float32),
    )


def thirds(values):
    first = values.astype(jnp.bfloat16).astype(jnp.float32)
    rest = values - first
    second = rest.astype(jnp.bfloat16).astype(jnp.float32)
    return jnp.concatenate([first, second, rest - second], axis=0).astype(jnp.bfloat16)


def add_thirds(parts):
    rows = parts.shape[0] // 3
    return parts[:rows] + parts[rows : 2 * rows] + parts[2 * rows :]


def spread_kernel(cells_ref, values_ref, out_ref):
    groups, rows, lanes = out_ref.shape
    slots = cells_ref.shape[1]
    index = lax.broadcasted_iota(jnp.int32, (slots, groups * lanes), 1)
    hits = jnp.where(index == cells_ref[0], 1.0, 0.0).astype(jnp.bfloat16)

    @pl.when(pl.program_id(0) == 0)
    def _():
        out_ref[...] = jnp.zeros_like(out_ref)

    parts = jnp.dot(thirds(values_ref[0]), hits, preferred_element_type=jnp.float32)
    whole = add_thirds(parts)
    for group in range(groups):
        out_ref[group] += whole[:rows, group * lanes : (group + 1) * lanes]


def pick_kernel(cells_ref, values_ref, out_ref):
    slots = cells_ref.shape[2]
    index = lax.broadcasted_iota(jnp.int32, (values_ref.shape[1], slots), 0)
    hits = jnp.where(index == cells_ref[0], 1.0, 0.0).astype(jnp.bfloat16)
    parts = jnp.dot(thirds(values_ref[...]), hits, preferred_element_type=jnp.float32)
    out_ref[0] = add_thirds(parts)[: out_ref.shape[1]]


def spread(cells, values, groups, lanes):
    sources, rows, slots = values.shape
    padded = -(-rows // 8) * 8
    values = jnp.pad(values, ((0, 0), (0, padded - rows), (0, 0)))
    return pl.pallas_call(
        spread_kernel,
        grid=(sources,),
        in_specs=[
            pl.BlockSpec((1, slots, 1), lambda i: (i, 0, 0)),
            pl.BlockSpec((1, padded, slots), lambda i: (i, 0, 0)),
        ],
        out_specs=pl.BlockSpec((groups, rows, lanes), lambda i: (0, 0, 0)),
        out_shape=jax.ShapeDtypeStruct((groups, rows, lanes), jnp.float32),
        compiler_params=pltpu.CompilerParams(vmem_limit_bytes=40 << 20),
    )(cells[:, :, None], values)


def pick(cells, values):
    sources, slots = cells.shape
    rows, count = values.shape
    padded = -(-rows // 8) * 8
    values = jnp.pad(values, ((0, padded - rows), (0, 0)))
    return pl.pallas_call(
        pick_kernel,
        grid=(sources,),
        in_specs=[
            pl.BlockSpec((1, 1, slots), lambda i: (i, 0, 0)),
            pl.BlockSpec((padded, count), lambda i: (0, 0)),
        ],
        out_specs=pl.BlockSpec((1, rows, slots), lambda i: (i, 0, 0)),
        out_shape=jax.ShapeDtypeStruct((sources, rows, slots), jnp.float32),
        compiler_params=pltpu.CompilerParams(vmem_limit_bytes=40 << 20),
    )(cells[:, None, :], values)


def product(left, right):
    return jnp.dot(left, right, precision=HIGHEST, preferred_element_type=jnp.float32)


def halves(values):
    first = values.astype(jnp.bfloat16)
    return first, (values - first.astype(jnp.float32)).astype(jnp.bfloat16)


def product_halves(left, right):
    def one(a, b):
        return jnp.dot(a, b, preferred_element_type=jnp.float32)

    return one(left[0], right[0]) + (one(left[0], right[1]) + one(left[1], right[0]))


def plane_kernel(layout, pitch, with_modulus, with_back, *refs):
    half, place, _ = layout
    arrived_ref, local_ref, inner_ref, outer_ref, lines_ref, back_ref = refs[:6]
    refs = refs[6:]
    if with_back:
        out_ref, refs = refs[0], refs[1:]
    if with_modulus:
        modulus_ref, refs = refs[0], refs[1:]
    box, cosine_part, sine_part = refs
    planes = local_ref.shape[0]
    rows = 2 * planes
    box[...] = jnp.zeros_like(box)
    for i in range(SIDE):
        device, lane = place[i]
        width = 2 * half[i] + 1
        box[i * pitch : i * pitch + rows, RAD - half[i] : RAD + half[i] + 1] = arrived_ref[
            device, :, lane : lane + width
        ]
    inner, outer = halves(inner_ref[...]), halves(outer_ref[...])
    turned = product_halves(halves(box[...]), halves(lines_ref[...]))
    cosine_part[...] = turned[:, :LANE]
    sine_part[...] = turned[:, LANE:]
    group = max(size for size in range(1, 5) if planes % size == 0)
    for begin in range(0, planes, group):
        top, bottom = [], []
        for p in range(begin, begin + group):
            real = pl.ds(p, KX, stride=pitch)
            imag = pl.ds(planes + p, KX, stride=pitch)
            line_real = cosine_part[real, :] - sine_part[imag, :]
            line_imag = sine_part[real, :] + cosine_part[imag, :]
            top += [line_real, line_imag]
            bottom += [-line_imag, line_real]
        lines = jnp.concatenate(
            [jnp.concatenate(top, axis=1), jnp.concatenate(bottom, axis=1)], axis=0
        )
        field = product_halves(inner, halves(lines))
        top, bottom = [], []
        for q in range(group):
            p = begin + q
            field_real = field[:, 2 * q * LANE : (2 * q + 1) * LANE]
            field_imag = field[:, (2 * q + 1) * LANE : (2 * q + 2) * LANE]
            if with_modulus:
                modulus_ref[p] = field_real * field_real + field_imag * field_imag
            if with_back:
                field_real = field_real * local_ref[p]
                field_imag = field_imag * local_ref[p]
                top += [field_real, field_imag]
                bottom += [field_imag, -field_real]
        if with_back:
            both = jnp.concatenate(
                [jnp.concatenate(top, axis=1), jnp.concatenate(bottom, axis=1)], axis=0
            )
            result = product_halves(outer, halves(both))
            result = jnp.concatenate(
                [result[:, 2 * q * LANE : (2 * q + 2) * LANE] for q in range(group)], axis=0
            )
            result = product_halves(halves(result), halves(back_ref[...]))
            for q in range(group):
                p = begin + q
                part = result[q * KX : (q + 1) * KX]
                box[pl.ds(p, KX, stride=pitch), :] = part[:, :LANE]
                box[pl.ds(planes + p, KX, stride=pitch), :] = part[:, LANE:]
    if with_back:
        out_ref[...] = jnp.zeros_like(out_ref)
        for i in range(SIDE):
            device, lane = place[i]
            width = 2 * half[i] + 1
            out_ref[device, :, lane : lane + width] = box[
                i * pitch : i * pitch + rows, RAD - half[i] : RAD + half[i] + 1
            ]


def plane_step(layout, arrived, local, tables, with_modulus, with_back):
    planes = local.shape[0]
    pitch = -(-2 * planes // 8) * 8
    shapes = []
    if with_back:
        shapes.append(jax.ShapeDtypeStruct(arrived.shape, jnp.float32))
    if with_modulus:
        shapes.append(jax.ShapeDtypeStruct(local.shape, jnp.float32))
    kernel = functools.partial(plane_kernel, layout, pitch, with_modulus, with_back)
    whole = pl.BlockSpec(memory_space=pltpu.VMEM)
    return pl.pallas_call(
        kernel,
        in_specs=[whole] * 6,
        out_specs=[whole] * len(shapes),
        out_shape=shapes,
        scratch_shapes=[pltpu.VMEM((KX * pitch, LANE), jnp.float32)] * 3,
        compiler_params=pltpu.CompilerParams(vmem_limit_bytes=40 << 20),
    )(arrived, local, *tables)


def trade(count, sent, landed, send_sem, recv_sem):
    me = lax.axis_index("plane")
    band = lax.axis_index("band")
    copies = []
    for k in range(1, count):
        partner = lax.rem(me + k, count)
        copy = pltpu.make_async_remote_copy(
            src_ref=sent.at[partner],
            dst_ref=landed.at[me],
            send_sem=send_sem.at[k - 1],
            recv_sem=recv_sem.at[k - 1],
            device_id=(band, partner),
            device_id_type=pl.DeviceIdType.MESH,
        )
        copy.start()
        copies.append(copy)
    landed[me] = sent[me]
    return copies


def greet(count):
    me = lax.axis_index("plane")
    band = lax.axis_index("band")
    barrier = pltpu.get_barrier_semaphore()
    for k in range(1, count):
        pl.semaphore_signal(
            barrier,
            inc=1,
            device_id=(band, lax.rem(me + k, count)),
            device_id_type=pl.DeviceIdType.MESH,
        )
    pl.semaphore_wait(barrier, count - 1)


def swap_kernel(count, sent_ref, out_ref, landed, send_sem, recv_sem):
    greet(count)
    for copy in trade(count, sent_ref, landed, send_sem, recv_sem):
        copy.wait()
    out_ref[...] = landed[...]


def swap(values, collective_id):
    count = values.shape[0]
    whole = pl.BlockSpec(memory_space=pltpu.VMEM)
    return pl.pallas_call(
        functools.partial(swap_kernel, count),
        in_specs=[whole],
        out_specs=whole,
        out_shape=jax.ShapeDtypeStruct(values.shape, jnp.float32),
        scratch_shapes=[pltpu.VMEM(values.shape, jnp.float32)]
        + [pltpu.SemaphoreType.DMA((count - 1,))] * 2,
        compiler_params=pltpu.CompilerParams(
            vmem_limit_bytes=40 << 20, collective_id=collective_id, has_side_effects=True
        ),
    )(values)


def height_kernel(count, factor, opening, last, *refs):
    spectrum_ref, term_ref, total_ref, kinetic_ref, inside_ref, table_ref, turned_ref = refs[:7]
    outs, scratch = refs[7 : 8 if last else 10], refs[8 if last else 10 :]
    landed, sent, final, flat, send_sem, recv_sem, send_later, recv_later = scratch[:8]
    greet(count)
    copies = trade(count, spectrum_ref, landed, send_sem, recv_sem)
    if opening:
        origin, origin_send, origin_recv = scratch[8:]
        copies += trade(count, term_ref, origin, origin_send, origin_recv)
    for copy in copies:
        copy.wait()
    rows = landed.shape[1]
    table, turned, inside = table_ref[...], turned_ref[...], inside_ref[...]

    def gathered(buffer):
        for d in range(count):
            flat[d * rows : (d + 1) * rows, :] = buffer[d]
        return product(turned, flat[...]) * inside

    before = gathered(origin) if opening else term_ref[...]
    total = before if opening else total_ref[...]
    applied = gathered(landed) + kinetic_ref[...] * before
    term = factor * jnp.concatenate([applied[KZ:], -applied[:KZ]], axis=0)
    total = total + term
    flat[...] = product(table, total if last else term)
    for d in range(count):
        sent[d] = flat[d * rows : (d + 1) * rows, :]
    copies = trade(count, sent, final, send_later, recv_later)
    if not last:
        outs[1][...] = term
        outs[2][...] = total
    for copy in copies:
        copy.wait()
    outs[0][...] = final[...]


def height_step(power, spectrum, term, total, kinetic, inside, table):
    count, rows, lanes = spectrum.shape
    opening, last = power == 1, power == 3
    shapes = [jax.ShapeDtypeStruct(spectrum.shape, jnp.float32)]
    if not last:
        shapes += [jax.ShapeDtypeStruct((table.shape[1], lanes), jnp.float32)] * 2
    whole = pl.BlockSpec(memory_space=pltpu.VMEM)
    block = pltpu.VMEM((count, rows, lanes), jnp.float32)
    marks = pltpu.SemaphoreType.DMA((count - 1,))
    return pl.pallas_call(
        functools.partial(height_kernel, count, TIMESTEP / power, opening, last),
        in_specs=[whole] * 7,
        out_specs=[whole] * len(shapes),
        out_shape=shapes,
        scratch_shapes=[block] * 3
        + [pltpu.VMEM((count * rows, lanes), jnp.float32)]
        + [marks] * 4
        + ([block, marks, marks] if opening else []),
        compiler_params=pltpu.CompilerParams(
            vmem_limit_bytes=40 << 20, collective_id=power, has_side_effects=True
        ),
    )(spectrum, term, total, kinetic, inside, table, np.ascontiguousarray(table.T))


def dot(subscripts, left, right):
    return jnp.einsum(subscripts, left, right, precision=HIGHEST)


def sum_bands(values):
    bands = lax.axis_size("band")
    if bands & (bands - 1):
        return lax.psum(values, "band")
    step = 1
    while step < bands:
        pairs = [(i, i ^ step) for i in range(bands)]
        values = values + lax.ppermute(values, "band", pairs)
        step *= 2
    return values


def shards(psi, potential, stick_column, stick_length):
    device_list = lax.axis_size("plane")
    planes = potential.shape[0]
    slots = stick_column.shape[0]
    layout = row_layout(device_list)
    half, place, lanes = layout
    wave = wave_table()
    shift, mask = height_tables(stick_length, planes, device_list)

    def exchange(values):
        return lax.all_to_all(values, "plane", split_axis=0, concat_axis=0, tiled=True)

    term = psi[:, 0] * mask
    upper = [
        dot("sj,jz->zs", term[0], wave[0]) - dot("sj,jz->zs", term[1], wave[1]),
        dot("sj,jz->zs", term[0], wave[1]) + dot("sj,jz->zs", term[1], wave[0]),
    ]
    upper = [part.reshape(device_list, planes, slots) for part in upper]
    first = signed(stick_column // NG)
    second = signed(stick_column % NG)
    base = np.array([place[i][0] * lanes + place[i][1] + half[i] for i in range(SIDE)], np.int32)
    chosen = first[None, :] + RAD == jnp.arange(SIDE, dtype=jnp.int32)[:, None]
    own_cell = jnp.sum(jnp.where(chosen, base[:, None], 0), axis=0) + second
    own_cell = jnp.where(stick_length > 0, own_cell, -1)
    packed = jnp.concatenate(
        [
            upper[0] * shift[0] - upper[1] * shift[1],
            upper[0] * shift[1] + upper[1] * shift[0],
            jnp.broadcast_to(own_cell.astype(jnp.float32), (device_list, 1, slots)),
        ],
        axis=1,
    )
    arrived = swap(packed, 4)
    cells = arrived[:, 2 * planes, :].astype(jnp.int32)
    start = spread(cells, arrived[:, : 2 * planes, :], device_list, lanes)

    local = jnp.pad(potential.reshape(planes, NG, NG), ((0, 0), (0, 0), (0, LANE - NG)))
    tables = plane_tables()
    table = height_table(planes, device_list)
    planar = np.full((device_list, lanes), 4 * RAD * RAD, np.int32)
    for i in range(SIDE):
        device, lane = place[i]
        spot = np.arange(-half[i], half[i] + 1)
        planar[device, lane : lane + 2 * half[i] + 1] = (i - RAD) ** 2 + spot * spot
    planar = lax.dynamic_slice_in_dim(jnp.asarray(planar), lax.axis_index("plane"), 1, 0)
    depth = np.concatenate([np.arange(KZ) - RAD] * 2).astype(np.int32)[:, None]
    square = planar + depth * depth
    inside = (square <= RAD * RAD).astype(jnp.float32)
    kinetic = square.astype(jnp.float32) / (RAD * RAD) * inside

    spectrum, before = plane_step(layout, start, local, tables, True, True)
    arrived, term, total = height_step(1, spectrum, start, kinetic, kinetic, inside, table)
    (spectrum,) = plane_step(layout, arrived, local, tables, False, True)
    arrived, term, total = height_step(2, spectrum, term, total, kinetic, inside, table)
    (spectrum,) = plane_step(layout, arrived, local, tables, False, True)
    (final,) = height_step(3, spectrum, term, total, kinetic, inside, table)
    (after,) = plane_step(layout, final, local, tables, True, False)
    final, after = lax.optimization_barrier((final, after))
    flat = final.transpose(1, 0, 2).reshape(2 * planes, device_list * lanes)
    home = exchange(pick(cells, flat))
    real, imag = home[:, :planes], home[:, planes:]
    turned = [
        (real * shift[0] + imag * shift[1]).reshape(NG, slots),
        (imag * shift[0] - real * shift[1]).reshape(NG, slots),
    ]
    psi_new = jnp.stack(
        [
            (dot("zs,jz->sj", turned[0], wave[0]) + dot("zs,jz->sj", turned[1], wave[1])) * mask,
            (dot("zs,jz->sj", turned[1], wave[0]) - dot("zs,jz->sj", turned[0], wave[1])) * mask,
        ]
    )[:, None]
    change = (after - before)[..., :NG].reshape(planes, NG * NG) / BAND_DEV
    whole = sum_bands(change)
    potential_new = potential + LINEAR_GAIN * whole + CUBIC_GAIN * whole * whole * whole
    return (psi_new, potential_new)


def solution(mesh):
    in_specs = (P(None, "band", "plane", None), P("plane", None), P("plane"), P("plane"))
    out_specs = (P(None, "band", "plane", None), P("plane", None))
    return jax.shard_map(shards, mesh=mesh, in_specs=in_specs, out_specs=out_specs, check_vma=False)
```
